256 devices in a mesh: lat: 64 (over y, z, x_hi), lon: 4 (over x_lo, core).
Axes of the slice: x: 4 (x_hi: 2, x_lo: 2; x = x_hi * 2 + x_lo), y: 4, z: 8, core: 2. Of those that a mesh axis runs over, the one named last changes fastest.
Arguments:
- features: bfloat16 [256, 128, 512], P(None, 'lat', 'lon'), may hold values from -6 to 6
- weight: bfloat16 [256, 2304], replicated, may hold values from -0.125 to 0.125
- filter_table: float32 [16, 9, 5], replicated, may hold values from -1.2 to 1.2
- row_range: int32 [128, 2], replicated, may hold values from 0 to 5, as said below
- basis_id: int32 [128, 5], replicated, may hold values from 0 to 15
- cotangent: bfloat16 [256, 128, 512], P(None, 'lat', 'lon'), may hold values from -6 to 6
Outputs:
- output: bfloat16 [256, 128, 512], P(None, 'lat', 'lon')
- input_grad: bfloat16 [256, 128, 512], P(None, 'lat', 'lon')
- weight_grad: float32 [256, 2304], replicated
The draws below stay inside these ranges and needn't reach their ends.
Inputs may be any that keep to these rules, and one draw needn't show every extreme that they name: `row_range`: column 0 never exceeds 2 and column 1 always exceeds 2; the first and last 2 rows use the whole window.
All inputs are finite; a program needn't handle non-finite values.
Results may differ from the reference program's by a relative error of at most 0.0059.
Values may be sent and summed in bfloat16 or wider, within the bound.
A program may use at most 128 MiB of HBM per device.

```python
import math
import jax
import jax.numpy as jnp
from jax import lax

CIN = 256
COUT = 256
K = 9
NB = 16
H = 2
LH = 2
R = 5
L = 5
NLAT = 128
NLON = 512


def draw_row_range(key, part):
    key = jax.random.fold_in(key, 7)
    first_key, second_key = jax.random.split(key)
    lower_end = jax.random.randint(first_key, (NLAT,), 0, H + 1)
    upper_end = jax.random.randint(second_key, (NLAT,), H + 1, 2 * H + 2)
    positions = jnp.arange(NLAT, dtype=jnp.int32)
    polar_rows = (positions < H) | (positions >= NLAT - H)
    lower_end = jnp.where(polar_rows, 0, lower_end)
    upper_end = jnp.where(polar_rows, 2 * H + 1, upper_end)
    return jnp.stack([lower_end, upper_end], axis=1).astype(jnp.int32)


def plant(drawn, key, smallest, top_value):
    extent = drawn.shape
    spot = [jax.random.randint(jax.random.fold_in(key, axis), (), 0, extent[axis]) for axis in range(len(extent))]
    drawn = drawn.at[tuple(spot)].set(smallest)
    longest = extent.index(max(extent))
    spot[longest] = (spot[longest] + 1) % extent[longest]
    return drawn.at[tuple(spot)].set(top_value)


def block_levels(key, extent, cuts, smallest, largest):
    gain, own = 1.0, jax.random.fold_in(key, 6)
    for dim, shards_of in cuts:
        draws = jnp.exp(jax.random.uniform(jax.random.fold_in(own, dim), (shards_of,), jnp.float32, smallest / len(cuts), largest / len(cuts)))
        gain = gain * jnp.repeat(draws, extent[dim] // shards_of).reshape([-1 if axis == dim else 1 for axis in range(len(extent))])
    return gain


def centred(stream_key, extent, scale, limit, cuts=(), held_as=jnp.bfloat16):
    drawn = scale * jax.random.normal(stream_key, extent, jnp.float32)
    if cuts:
        drawn = drawn * block_levels(stream_key, extent, cuts, -0.22, 0.18)
    return jnp.clip(drawn, -limit, limit).astype(held_as)


def setup_inputs(seed: int = 0) -> dict:
    seeds = jax.random.split(jax.random.key(seed), 7)
    features = centred(seeds[0], (CIN, NLAT, NLON), 1.0, 6.0, ((1, 64), (2, 4)))
    weight = centred(seeds[1], (COUT, CIN * K), (CIN * K) ** -0.5, 0.125)
    filter_table = centred(seeds[2], (NB, K, L), 0.2, 1.2, (), jnp.float32)
    row_range = draw_row_range(jax.random.fold_in(seeds[6], 71), 0)
    basis_id = plant(jax.random.randint(seeds[4], (NLAT, R), 0, NB), jax.random.fold_in(seeds[4], 1), 0, NB - 1).astype(jnp.int32)
    cotangent = centred(seeds[5], (COUT, NLAT, NLON), 1.0, 6.0, ((1, 64), (2, 4)))
    return {"features": features, "weight": weight, "filter_table": filter_table, "row_range": row_range, "basis_id": basis_id, "cotangent": cotangent}


def coefficients(filter_table, row_range, basis_id):
    shapes = filter_table.shape[0]
    onehot = (basis_id[:, :, None] == jnp.arange(shapes, dtype=jnp.int32)[None, None, :]).astype(jnp.float32)
    lookup = jnp.einsum('tjb,bkl->tkjl', onehot, filter_table, precision=lax.Precision.HIGHEST)
    offsets = jnp.arange(basis_id.shape[1], dtype=jnp.int32)
    active = (offsets[None, :] >= row_range[:, 0:1]) & (offsets[None, :] < row_range[:, 1:2])
    return (lookup * active[:, None, :, None].astype(jnp.float32)).astype(jnp.bfloat16)

def reference(features, weight, filter_table, row_range, basis_id, cotangent):
    filter_coef = coefficients(filter_table, row_range, basis_id)
    channels = features.shape[0]
    out_channels = weight.shape[0]
    padded = jnp.pad(features, ((0, 0), (H, H), (0, 0)))
    padded = jnp.concatenate([padded[:, :, NLON - LH:], padded, padded[:, :, :LH]], axis=2)

    def row_step(state_pair, t):
        grad_sum, grad_pad = state_pair
        window = lax.dynamic_slice_in_dim(padded, t, R, 1)
        stacked = jnp.stack([window[:, :, l:l + NLON] for l in range(L)], axis=2)
        row_coef = lax.dynamic_index_in_dim(filter_coef, t, 0, keepdims=False)
        basis_out = jnp.einsum('cjlp,kjl->ckp', stacked.astype(jnp.float32), row_coef.astype(jnp.float32)).astype(jnp.bfloat16)
        flat_basis = basis_out.reshape(channels * K, NLON)
        out_row = jnp.dot(weight, flat_basis, preferred_element_type=jnp.float32).astype(jnp.bfloat16)
        cot_row = lax.dynamic_index_in_dim(cotangent, t, 1, keepdims=False)
        grad_sum = grad_sum + lax.dot_general(cot_row, flat_basis, (((1,), (1,)), ((), ())), preferred_element_type=jnp.float32)
        basis_grad = lax.dot_general(weight, cot_row, (((0,), (0,)), ((), ())), preferred_element_type=jnp.float32).astype(jnp.bfloat16).reshape(channels, K, NLON)
        contrib = jnp.einsum('ckp,kjl->cjlp', basis_grad.astype(jnp.float32), row_coef.astype(jnp.float32))
        spread = jnp.zeros((channels, R, NLON + 2 * LH), jnp.float32)
        for l in range(L):
            spread = spread + jnp.pad(contrib[:, :, l], ((0, 0), (0, 0), (l, 2 * LH - l)))
        previous = lax.dynamic_slice_in_dim(grad_pad, t, R, 1)
        grad_pad = lax.dynamic_update_slice_in_dim(grad_pad, previous + spread, t, 1)
        return ((grad_sum, grad_pad), out_row)
    start_pair = (jnp.zeros((out_channels, channels * K), jnp.float32), jnp.zeros((channels, NLAT + 2 * H, NLON + 2 * LH), jnp.float32))
    (grad_sum, grad_pad), out_rows = lax.scan(row_step, start_pair, jnp.arange(NLAT, dtype=jnp.int32))
    output = jnp.transpose(out_rows, (1, 0, 2))
    middle = grad_pad[:, H:H + NLAT]
    center = middle[:, :, LH:LH + NLON]
    center = center.at[:, :, NLON - LH:].add(middle[:, :, :LH])
    center = center.at[:, :, :LH].add(middle[:, :, LH + NLON:])
    input_grad = center.astype(jnp.bfloat16)
    weight_grad = grad_sum * jnp.float32(1.0 / math.sqrt(NLAT * NLON))
    return (output, input_grad, weight_grad)
```

```python
import functools
import math

import jax
import jax.numpy as jnp
from jax import lax
from jax.experimental import pallas as pl
from jax.experimental.pallas import tpu as pltpu
from jax.sharding import PartitionSpec as P

BF = jnp.bfloat16
F32 = jnp.float32
MESH = pl.DeviceIdType.MESH
C = 256
K = 9
LANES = 128
NY, NZ, NX = 4, 8, 4
NXY = NX * NY
N_LAT, N_LON = 64, 4
N_ROWS = 128
PIECE = 144
ZROWS = 18
ZPAD = 32
NT = (((1,), (1,)), ((), ()))
TN = (((0,), (0,)), ((), ()))
NN = (((1,), (0,)), ((), ()))


def dot(a, b, dims=NN):
    return lax.dot_general(a, b, dims, preferred_element_type=F32)


def kernel(
    feat, cot, w, table, rng, ids,
    out, ig, wg,
    fx, e_send, e_recv, bmat, bhal, big, bo, bgk, igp, gr, egs, egr,
    cs, cr, own, xs, xr, zf, zs, zr, gz, ga,
    f_ss, f_rs, e_ss, e_rs, g_ss, g_rs, h_ss, h_rs, c_ss, c_rs,
    x_ss, x_rs, z_ss, z_rs, gz_ss, gz_rs, gx_ss, gx_rs, gc_ss, gc_rs,
):
    la, lo = lax.axis_index("lat"), lax.axis_index("lon")
    y, z, xh = la // 16, (la // 2) % 8, la % 2
    xl, core = lo // 2, lo % 2
    x = xh * 2 + xl
    me_n = y * 4 + x
    sibling = (la, lo + 1 - 2 * core)

    def lat_peer(dl):
        return (lax.rem(la + dl + N_LAT, N_LAT), lo)

    def edge_peer(s):
        dl, dc = s // 2 - 1, 2 * (s % 2) - 1
        return (lax.rem(la + dl + N_LAT, N_LAT), lax.rem(lo + dc + N_LON, N_LON))

    def xy_peer(i):
        py, px = (y + i // 4) % 4, (x + i % 4) % 4
        return ((py * 8 + z) * 2 + px // 2, (px % 2) * 2 + core)

    def z_peer(i):
        return ((y * 8 + (z + i) % 8) * 2 + xh, lo)

    barrier = pltpu.get_barrier_semaphore()

    def greet(peer):
        pl.semaphore_signal(barrier, inc=1, device_id=peer, device_id_type=MESH)

    greet(lat_peer(-1))
    greet(lat_peer(1))
    for s in range(6):
        greet(edge_peer(s))
    greet(sibling)

    def greet_xy(i, _):
        greet(xy_peer(i))
        return 0

    def greet_z(i, _):
        greet(z_peer(i))
        return 0

    lax.fori_loop(1, NXY, greet_xy, 0)
    lax.fori_loop(1, NZ, greet_z, 0)

    rho = lax.broadcasted_iota(jnp.int32, (16, 2 * LANES), 0)
    col = lax.broadcasted_iota(jnp.int32, (16, 2 * LANES), 1)
    edge_i = rho % 4
    edge_col = jnp.where(edge_i < 2, edge_i, edge_i + LANES - 4)
    sel = ((rho < 8) & (col == (rho // 4) * LANES + edge_col)).astype(F32).astype(BF)
    e_send[...] = dot(sel, feat[...], NT).astype(BF)

    pl.semaphore_wait(barrier, 2 + 6 + 1 + (NXY - 1) + (NZ - 1))

    def remote(src, dst, ss, rs, peer):
        return pltpu.make_async_remote_copy(
            src_ref=src, dst_ref=dst, send_sem=ss, recv_sem=rs, device_id=peer, device_id_type=MESH
        )

    feat_copies = [
        remote(feat, fx.at[1], f_ss.at[0], f_rs.at[1], lat_peer(-1)),
        remote(feat, fx.at[0], f_ss.at[1], f_rs.at[0], lat_peer(1)),
    ]
    for c in feat_copies:
        c.start()
    edge_copies = [
        remote(e_send, e_recv.at[5 - s], e_ss.at[s], e_rs.at[5 - s], edge_peer(s)) for s in range(6)
    ]
    for c in edge_copies:
        c.start()

    diag = lax.broadcasted_iota(jnp.int32, (LANES, LANES), 0) - lax.broadcasted_iota(
        jnp.int32, (LANES, LANES), 1
    ) + 2
    hr = lax.broadcasted_iota(jnp.int32, (16, LANES), 0)
    hp = lax.broadcasted_iota(jnp.int32, (16, LANES), 1)
    row_ids, row_act = [], []
    for t in range(2):
        g = la * 2 + t
        r0, r1 = rng[0, g], rng[1, g]
        row_ids.append([ids[j, g] for j in range(5)])
        row_act.append(
            [
                (j >= r0) & (j < r1) & (g + j - 2 >= 0) & (g + j - 2 < N_ROWS)
                for j in range(5)
            ]
        )
    zero_block = jnp.zeros((LANES, LANES), BF)

    def build(k, _):
        coef = [
            [
                [jnp.where(row_act[t][j], table[k, l, row_ids[t][j]], 0.0) for l in range(5)]
                for j in range(5)
            ]
            for t in range(2)
        ]
        for t in range(2):
            lanes = slice(t * LANES, (t + 1) * LANES)
            for e in range(6):
                j = e - t
                rows = slice((e % 2) * LANES, (e % 2 + 1) * LANES)
                if j < 0 or j > 4:
                    bmat[k, e // 2, rows, lanes] = zero_block
                    continue
                v = jnp.zeros((LANES, LANES), F32)
                for l in range(5):
                    v = jnp.where(diag == l, coef[t][j][l], v)
                bmat[k, e // 2, rows, lanes] = v.astype(BF)
            for s in range(6):
                v = jnp.zeros((16, LANES), F32)
                for r in range(2):
                    j = (s // 2) * 2 + r - t
                    if j < 0 or j > 4:
                        continue
                    if s % 2 == 0:
                        outer = (hr == r * 4 + 2) & (hp == 0) | (hr == r * 4 + 3) & (hp == 1)
                        inner = (hr == r * 4 + 3) & (hp == 0)
                        v = jnp.where(outer, coef[t][j][0], jnp.where(inner, coef[t][j][1], v))
                    else:
                        outer = (hr == r * 4) & (hp == 126) | (hr == r * 4 + 1) & (hp == 127)
                        inner = (hr == r * 4) & (hp == 127)
                        v = jnp.where(outer, coef[t][j][4], jnp.where(inner, coef[t][j][3], v))
                bhal[k, s * 16 : s * 16 + 16, lanes] = v.astype(BF)
        return 0

    lax.fori_loop(0, K, build, 0)

    def basis_grad(m, _):
        cols = pl.ds(pl.multiple_of(m * 256, 256), 256)
        g = dot(w[:, cols], cot[...], TN)
        big[0, cols, :] = g[:, :LANES]
        big[1, cols, :] = g[:, LANES:]
        return 0

    lax.fori_loop(0, K, basis_grad, 0)
    for k in range(K):
        for t in range(2):
            bgk[k, :, t * LANES : (t + 1) * LANES] = big[t, pl.ds(k, C, stride=K), :].astype(BF)

    def input_grad(dl):
        acc = dot(bgk[0], bmat[0, dl], NT)
        for k in range(1, K):
            acc += dot(bgk[k], bmat[k, dl], NT)
        return acc

    igp[0] = input_grad(0).astype(BF)
    igp[1] = input_grad(2).astype(BF)
    acc = dot(bhal[0], bgk[0], NT)
    for k in range(1, K):
        acc += dot(bhal[k], bgk[k], NT)
    for s in range(6):
        egs[s] = acc[s * 16 : s * 16 + 16].astype(BF)
    grad_copies = [
        remote(igp.at[0], gr.at[1], g_ss.at[0], g_rs.at[1], lat_peer(-1)),
        remote(igp.at[1], gr.at[0], g_ss.at[1], g_rs.at[0], lat_peer(1)),
    ] + [remote(egs.at[s], egr.at[s], h_ss.at[s], h_rs.at[s], edge_peer(s)) for s in range(6)]
    for c in grad_copies:
        c.start()

    for c in feat_copies + edge_copies:
        c.wait()
    halo = e_recv[...].reshape(96, C)
    for k in range(K):
        acc = dot(feat[...], bmat[k, 1]) + dot(fx[0], bmat[k, 0]) + dot(fx[1], bmat[k, 2])
        acc += dot(halo, bhal[k], TN)
        big[0, pl.ds(k, C, stride=K), :] = acc[:, :LANES]
        big[1, pl.ds(k, C, stride=K), :] = acc[:, LANES:]

    def to_tiles(v):
        return jnp.concatenate(
            [v[:, :LANES].reshape(16, 8, LANES), v[:, LANES:].reshape(16, 8, LANES)], axis=1
        )

    theirs = cot[pl.ds(pl.multiple_of(128 * (1 - core), 128), 128), :]
    mine = cot[pl.ds(pl.multiple_of(128 * core, 128), 128), :]
    for m in range(K):
        rows = slice(m * 256, m * 256 + 256)
        bo[rows, :LANES] = big[0, rows, :].astype(BF)
        bo[rows, LANES:] = big[1, rows, :].astype(BF)
        cs[:, m * 16 : m * 16 + 16, :] = to_tiles(dot(theirs, bo[rows, :], NT)).astype(BF)
    core_copy = remote(cs, cr, c_ss, c_rs, sibling)
    core_copy.start()
    for m in range(K):
        rows = slice(m * 256, m * 256 + 256)
        own[:, m * 16 : m * 16 + 16, :] = to_tiles(dot(mine, bo[rows, :], NT))
    core_copy.wait()

    def reduce_core(n, _):
        xs[n] = (own[n] + cr[n].astype(F32)).astype(BF)
        return 0

    lax.fori_loop(0, NXY, reduce_core, 0)

    def xy_index(i):
        return ((y + i // 4) % 4) * 4 + (x + i % 4) % 4

    def xy_copy(i):
        return remote(xs.at[xy_index(i)], xr.at[i], x_ss.at[i], x_rs.at[i], xy_peer(i))

    def xy_start(i, _):
        xy_copy(i).start()
        return 0

    lax.fori_loop(1, NXY, xy_start, 0)

    acc = dot(w[:, :256], bo[:256, :])
    for m in range(1, K):
        acc += dot(w[:, m * 256 : m * 256 + 256], bo[m * 256 : m * 256 + 256, :])
    out[...] = acc.astype(BF)

    def xy_add(i, total):
        xy_copy(i).wait()
        return total + xr[i].astype(F32)

    zf[0:PIECE, :] = lax.fori_loop(1, NXY, xy_add, xs[me_n].astype(F32))
    zf[PIECE:, :] = jnp.zeros((ZPAD - ZROWS + 2, LANES), F32)
    for i in range(NZ):
        zs[i] = zf[ZROWS * i : ZROWS * i + ZPAD, :].astype(BF)

    def z_copy(i):
        return remote(zs.at[(z + i) % 8], zr.at[i], z_ss.at[i], z_rs.at[i], z_peer(i))

    def z_start(i, _):
        z_copy(i).start()
        return 0

    def z_add(i, total):
        z_copy(i).wait()
        return total + zr[i].astype(F32)

    lax.fori_loop(1, NZ, z_start, 0)
    total = lax.fori_loop(1, NZ, z_add, zs[z].astype(F32))
    gz[z] = (total * F32(1.0 / math.sqrt(N_ROWS * N_LON * LANES))).astype(BF)

    def gz_copy(i):
        return remote(gz.at[z], gz.at[z], gz_ss.at[i], gz_rs.at[i], z_peer(i))

    def gz_landed(i):
        src = (z + 8 - i) % 8
        return remote(gz.at[src], gz.at[src], gz_ss.at[i], gz_rs.at[i], z_peer(i))

    def gz_start(i, _):
        gz_copy(i).start()
        return 0

    def gz_wait(i, _):
        gz_copy(i).wait_send()
        gz_landed(i).wait_recv()
        return 0

    lax.fori_loop(1, NZ, gz_start, 0)
    lax.fori_loop(1, NZ, gz_wait, 0)
    for i in range(NZ):
        zf[ZROWS * i : ZROWS * i + ZPAD, :] = gz[i].astype(F32)
    ga[core, me_n] = zf[0:PIECE, :].astype(BF)

    def gx_copy(i):
        return remote(ga.at[core, me_n], ga.at[core, me_n], gx_ss.at[i], gx_rs.at[i], xy_peer(i))

    def from_index(i):
        return ((y + 4 - i // 4) % 4) * 4 + (x + 4 - i % 4) % 4

    def gx_landed(i):
        n = from_index(i)
        return remote(ga.at[core, n], ga.at[core, n], gx_ss.at[i], gx_rs.at[i], xy_peer(i))

    def gc_copy(i):
        n = from_index(i)
        return remote(ga.at[core, n], ga.at[core, n], gc_ss.at[i], gc_rs.at[i], sibling)

    def gc_landed(i):
        n = from_index(i)
        return remote(ga.at[1 - core, n], ga.at[1 - core, n], gc_ss.at[i], gc_rs.at[i], sibling)

    def gx_start(i, _):
        gx_copy(i).start()
        return 0

    def gx_pass(i, _):
        gx_landed(i).wait_recv()
        gc_copy(i).start()
        return 0

    lax.fori_loop(1, NXY, gx_start, 0)
    gc_copy(0).start()

    for c in grad_copies:
        c.wait()
    edges = egr[0].astype(F32)
    for s in range(1, 6):
        edges += egr[s].astype(F32)
    acc = input_grad(1) + gr[0].astype(F32) + gr[1].astype(F32)
    edge_hi = edges.astype(BF)
    edge_lo = (edges - edge_hi.astype(F32)).astype(BF)
    acc += dot(edge_hi, sel, TN) + dot(edge_lo, sel, TN)
    ig[...] = acc.astype(BF)

    lax.fori_loop(1, NXY, gx_pass, 0)

    def gx_drain(i, _):
        gx_copy(i).wait_send()
        return 0

    def gc_drain(i, _):
        gc_copy(i).wait_send()
        gc_landed(i).wait_recv()
        return 0

    lax.fori_loop(0, NXY, gc_drain, 0)
    lax.fori_loop(1, NXY, gx_drain, 0)

    for h in range(2):
        for m in range(K):
            v = ga[h, :, m * 16 : m * 16 + 16, :].astype(F32)
            rows = slice(h * 128, h * 128 + 128)
            wg[rows, m * 256 : m * 256 + LANES] = v[:, :8].reshape(128, LANES)
            wg[rows, m * 256 + LANES : m * 256 + 256] = v[:, 8:].reshape(128, LANES)


def per_device(features, weight, filter_table, row_range, basis_id, cotangent):
    vmem = pl.BlockSpec(memory_space=pltpu.VMEM)
    smem = pl.BlockSpec(memory_space=pltpu.SMEM)
    dma = pltpu.SemaphoreType.DMA
    scratch = [
        pltpu.VMEM((2, C, 256), BF),
        pltpu.VMEM((16, C), BF),
        pltpu.VMEM((6, 16, C), BF),
        pltpu.VMEM((K, 3, 256, 256), BF),
        pltpu.VMEM((K, 96, 256), BF),
        pltpu.VMEM((2, C * K, LANES), F32),
        pltpu.VMEM((C * K, 256), BF),
        pltpu.VMEM((K, C, 256), BF),
        pltpu.VMEM((2, C, 256), BF),
        pltpu.VMEM((2, C, 256), BF),
        pltpu.VMEM((6, 16, C), BF),
        pltpu.VMEM((6, 16, C), BF),
        pltpu.VMEM((NXY, PIECE, LANES), BF),
        pltpu.VMEM((NXY, PIECE, LANES), BF),
        pltpu.VMEM((NXY, PIECE, LANES), F32),
        pltpu.VMEM((NXY, PIECE, LANES), BF),
        pltpu.VMEM((NXY, PIECE, LANES), BF),
        pltpu.VMEM((PIECE + ZPAD - ZROWS + 2, LANES), F32),
        pltpu.VMEM((NZ, ZPAD, LANES), BF),
        pltpu.VMEM((NZ, ZPAD, LANES), BF),
        pltpu.VMEM((NZ, ZPAD, LANES), BF),
        pltpu.VMEM((2, NXY, PIECE, LANES), BF),
        dma((2,)), dma((2,)), dma((6,)), dma((6,)), dma((2,)), dma((2,)), dma((6,)), dma((6,)),
        dma, dma, dma((NXY,)), dma((NXY,)), dma((NZ,)), dma((NZ,)), dma((NZ,)), dma((NZ,)),
        dma((NXY,)), dma((NXY,)), dma((NXY,)), dma((NXY,)),
    ]
    out, ig, wg = pl.pallas_call(
        kernel,
        out_shape=(
            jax.ShapeDtypeStruct((C, 256), BF),
            jax.ShapeDtypeStruct((C, 256), BF),
            jax.ShapeDtypeStruct((C, C * K), F32),
        ),
        in_specs=[vmem, vmem, vmem, smem, smem, smem],
        out_specs=(vmem, vmem, vmem),
        scratch_shapes=scratch,
        compiler_params=pltpu.CompilerParams(
            collective_id=0, has_side_effects=True, vmem_limit_bytes=56 * 1024 * 1024
        ),
    )(
        features.reshape(C, 256),
        cotangent.reshape(C, 256),
        weight,
        filter_table.transpose(1, 2, 0),
        row_range.T,
        basis_id.T,
    )
    return out.reshape(C, 2, LANES), ig.reshape(C, 2, LANES), wg


def solution(mesh):
    in_specs = (P(None, "lat", "lon"), P(), P(), P(), P(), P(None, "lat", "lon"))
    out_specs = (P(None, "lat", "lon"), P(None, "lat", "lon"), P())
    return jax.shard_map(
        per_device, mesh=mesh, in_specs=in_specs, out_specs=out_specs, check_vma=False
    )
```

```python
import functools
import math

import jax
import jax.numpy as jnp
from jax import lax
from jax.experimental import pallas as pl
from jax.experimental.pallas import tpu as pltpu
from jax.sharding import PartitionSpec as P

BF = jnp.bfloat16
F32 = jnp.float32
MESH = pl.DeviceIdType.MESH
C = 256
K = 9
LANES = 128
NZ = 8
N_LAT, N_LON = 64, 4
N_ROWS = 128
HALF = C * K // 2
TILES = HALF // LANES
NT = (((1,), (1,)), ((), ()))
TN = (((0,), (0,)), ((), ()))
NN = (((1,), (0,)), ((), ()))


def dot(a, b, dims=NN):
    return lax.dot_general(a, b, dims, preferred_element_type=F32)


def kernel(
    feat, cot, w_hbm, table, rng, ids,
    out, ig, wg,
    w, fx, e_send, e_recv, bmat, bhal, big, bo, bgk, igp, gr, egs, egr,
    cs, cr, own, s1, r1, zf, s2, r2, zg, s3, r3, g1, g2,
    w_sem, f_ss, f_rs, e_ss, e_rs, g_ss, g_rs, h_ss, h_rs, c_ss, c_rs,
    s1_ss, s1_rs, s2_ss, s2_rs, s3_ss, s3_rs,
    g1_ss, g1_rs, g2_ss, g2_rs, g3_ss, g3_rs, gc_ss, gc_rs,
):
    la, lo = lax.axis_index("lat"), lax.axis_index("lon")
    y, z, xh = la // 16, (la // 2) % 8, la % 2
    xl, core = lo // 2, lo % 2
    x = xh * 2 + xl
    sibling = (la, lo + 1 - 2 * core)
    me1, me2 = (y, x), (x, y)

    def lat_peer(dl):
        return (lax.rem(la + dl + N_LAT, N_LAT), lo)

    def edge_peer(s):
        dl, dc = s // 2 - 1, 2 * (s % 2) - 1
        return (lax.rem(la + dl + N_LAT, N_LAT), lax.rem(lo + dc + N_LON, N_LON))

    def y_peer(i):
        return ((((y + i) % 4) * 8 + z) * 2 + xh, lo)

    def x_peer(i):
        px = (x + i) % 4
        return ((y * 8 + z) * 2 + px // 2, (px % 2) * 2 + core)

    def z_peer(i):
        return ((y * 8 + (z + i) % 8) * 2 + xh, lo)

    peer1, peer2 = (y_peer, x_peer), (x_peer, y_peer)

    barrier = pltpu.get_barrier_semaphore()
    peers = [lat_peer(-1), lat_peer(1)] + [edge_peer(s) for s in range(6)]
    peers += [y_peer(i) for i in (1, 2, 3)] + [x_peer(i) for i in (1, 3)]
    peers += [z_peer(i) for i in range(1, NZ)]
    for peer in peers:
        pl.semaphore_signal(barrier, inc=1, device_id=peer, device_id_type=MESH)
    w_copy = pltpu.make_async_copy(w_hbm, w, w_sem)
    w_copy.start()

    rho = lax.broadcasted_iota(jnp.int32, (16, 2 * LANES), 0)
    col = lax.broadcasted_iota(jnp.int32, (16, 2 * LANES), 1)
    edge_i = rho % 4
    edge_col = jnp.where(edge_i < 2, edge_i, edge_i + LANES - 4)
    sel = ((rho < 8) & (col == (rho // 4) * LANES + edge_col)).astype(F32).astype(BF)
    e_send[...] = dot(sel, feat[...], NT).astype(BF)

    pl.semaphore_wait(barrier, len(peers))

    def remote(src, dst, ss, rs, peer):
        return pltpu.make_async_remote_copy(
            src_ref=src, dst_ref=dst, send_sem=ss, recv_sem=rs, device_id=peer, device_id_type=MESH
        )

    half_rows = [slice(0, 128), slice(128, 256)]
    feat_copies = [
        [
            remote(
                feat.at[half_rows[h]], fx.at[1, half_rows[h]], f_ss.at[h, 0], f_rs.at[h, 1], lat_peer(-1)
            ),
            remote(
                feat.at[half_rows[h]], fx.at[0, half_rows[h]], f_ss.at[h, 1], f_rs.at[h, 0], lat_peer(1)
            ),
        ]
        for h in range(2)
    ]
    edge_copies = [
        remote(e_send, e_recv.at[5 - s], e_ss.at[s], e_rs.at[5 - s], edge_peer(s)) for s in range(6)
    ]
    for c in feat_copies[0] + edge_copies + feat_copies[1]:
        c.start()

    diag = lax.broadcasted_iota(jnp.int32, (LANES, LANES), 0) - lax.broadcasted_iota(
        jnp.int32, (LANES, LANES), 1
    ) + 2
    hr = lax.broadcasted_iota(jnp.int32, (16, LANES), 0)
    hp = lax.broadcasted_iota(jnp.int32, (16, LANES), 1)
    row_ids, row_act = [], []
    for t in range(2):
        g = la * 2 + t
        r0, r1_ = rng[0, g], rng[1, g]
        row_ids.append([ids[j, g] for j in range(5)])
        row_act.append(
            [
                (j >= r0) & (j < r1_) & (g + j - 2 >= 0) & (g + j - 2 < N_ROWS)
                for j in range(5)
            ]
        )
    zero_block = jnp.zeros((LANES, LANES), BF)

    def build(k, _):
        coef = [
            [
                [jnp.where(row_act[t][j], table[k, l, row_ids[t][j]], 0.0) for l in range(5)]
                for j in range(5)
            ]
            for t in range(2)
        ]
        for t in range(2):
            lanes = slice(t * LANES, (t + 1) * LANES)
            for e in range(6):
                j = e - t
                rows = slice((e % 2) * LANES, (e % 2 + 1) * LANES)
                if j < 0 or j > 4:
                    bmat[k, e // 2, rows, lanes] = zero_block
                    continue
                v = jnp.zeros((LANES, LANES), F32)
                for l in range(5):
                    v = jnp.where(diag == l, coef[t][j][l], v)
                bmat[k, e // 2, rows, lanes] = v.astype(BF)
            for s in range(6):
                v = jnp.zeros((16, LANES), F32)
                for r in range(2):
                    j = (s // 2) * 2 + r - t
                    if j < 0 or j > 4:
                        continue
                    if s % 2 == 0:
                        outer = (hr == r * 4 + 2) & (hp == 0) | (hr == r * 4 + 3) & (hp == 1)
                        inner = (hr == r * 4 + 3) & (hp == 0)
                        v = jnp.where(outer, coef[t][j][0], jnp.where(inner, coef[t][j][1], v))
                    else:
                        outer = (hr == r * 4) & (hp == 126) | (hr == r * 4 + 1) & (hp == 127)
                        inner = (hr == r * 4) & (hp == 127)
                        v = jnp.where(outer, coef[t][j][4], jnp.where(inner, coef[t][j][3], v))
                bhal[k, s * 16 : s * 16 + 16, lanes] = v.astype(BF)
        return 0

    lax.fori_loop(0, K, build, 0)
    for h in range(2):
        zf[h, :, 72:80, :] = jnp.zeros((4, 8, LANES), F32)

    theirs = pl.ds(pl.multiple_of(128 * (1 - core), 128), 128)
    mine = pl.ds(pl.multiple_of(128 * core, 128), 128)
    chunks = [(0, 256), (256, 512), (512, 768), (768, 1024), (1024, 1152)]

    def core_copy(h):
        return remote(cs.at[h], cr.at[h], c_ss.at[h], c_rs.at[h], sibling)

    def basis(h):
        hc = half_rows[h]
        halo = e_recv[:, :, hc].reshape(96, 128)
        for k in range(K):
            acc = dot(feat[hc, :], bmat[k, 1]) + dot(fx[0, hc, :], bmat[k, 0])
            acc += dot(fx[1, hc, :], bmat[k, 2]) + dot(halo, bhal[k], TN)
            rows = pl.ds(h * HALF + k, 128, stride=K)
            big[0, rows, :] = acc[:, :LANES]
            big[1, rows, :] = acc[:, LANES:]
        for a, b in chunks:
            rows = slice(h * HALF + a, h * HALF + b)
            bo[rows, :LANES] = big[0, rows, :].astype(BF)
            bo[rows, LANES:] = big[1, rows, :].astype(BF)
            cs[h, :, a:b] = dot(cot[theirs, :], bo[rows, :], NT).astype(BF)
        core_copy(h).start()

    def weight_rows(h):
        for a, b in chunks:
            own[h, :, a:b] = dot(cot[mine, :], bo[h * HALF + a : h * HALF + b, :], NT)

    def s1_copy(h, i):
        rows = pl.ds(pl.multiple_of(32 * ((me1[h] + i) % 4), 32), 32)
        return remote(s1.at[h, rows], r1.at[h, i], s1_ss.at[h, i], s1_rs.at[h, i], peer1[h](i))

    def s2_copy(h, i):
        n = (me2[h] + i) % 4
        return remote(s2.at[h, n], r2.at[h, i], s2_ss.at[h, i], s2_rs.at[h, i], peer2[h](i))

    def s3_copy(h, i):
        n = (z + i) % 8
        return remote(s3.at[h, n], r3.at[h, i], s3_ss.at[h, i], s3_rs.at[h, i], z_peer(i))

    def g1_copy(h, i, n):
        return remote(g1.at[h, n], g1.at[h, n], g1_ss.at[h, i], g1_rs.at[h, i], z_peer(i))

    def g2_copy(h, i, n):
        return remote(g2.at[h, n], g2.at[h, n], g2_ss.at[h, i], g2_rs.at[h, i], peer2[h](i))

    def piece(h, c, n):
        rows = pl.ds(pl.multiple_of(128 * c + 32 * n, 32), 32)
        return wg.at[rows, h * HALF : (h + 1) * HALF]

    def g3_copy(h, i, n):
        ref = piece(h, core, n)
        return remote(ref, ref, g3_ss.at[h, i], g3_rs.at[h, i], peer1[h](i))

    def gc_copy(h, i, c, n):
        ref = piece(h, c, n)
        return remote(ref, ref, gc_ss.at[h, i], gc_rs.at[h, i], sibling)

    def core_sum(h):
        core_copy(h).wait()
        s1[h] = (own[h] + cr[h].astype(F32)).astype(BF)
        for i in (1, 2, 3):
            s1_copy(h, i).start()

    def sum1(h):
        rows = pl.ds(pl.multiple_of(32 * me1[h], 32), 32)
        total = s1[h, rows, :].astype(F32)
        for i in (1, 2, 3):
            s1_copy(h, i).wait()
            total += r1[h, i].astype(F32)
        for m in range(TILES):
            tile = total[:, m * LANES : (m + 1) * LANES]
            zf[h, :, 8 * m : 8 * m + 8, :] = tile.reshape(4, 8, LANES)
        s2[h] = zf[h].astype(BF)
        for i in (1, 2, 3):
            s2_copy(h, i).start()

    def sum2(h):
        total = s2[h, me2[h]].astype(F32)
        for i in (1, 2, 3):
            s2_copy(h, i).wait()
            total += r2[h, i].astype(F32)
        zg[h] = total
        for i in range(NZ):
            s3[h, i] = zg[h, 9 * i : 9 * i + 16, :].astype(BF)
        for i in range(1, NZ):
            s3_copy(h, i).start()

    def sum3(h):
        total = s3[h, z].astype(F32)
        for i in range(1, NZ):
            s3_copy(h, i).wait()
            total += r3[h, i].astype(F32)
        g1[h, z] = (total * F32(1.0 / math.sqrt(N_ROWS * N_LON * LANES))).astype(BF)
        for i in range(1, NZ):
            g1_copy(h, i, z).start()

    def gather1(h):
        for i in range(1, NZ):
            g1_copy(h, i, z).wait_send()
            g1_copy(h, i, (z + 8 - i) % 8).wait_recv()
        for i in range(NZ):
            zg[h, 9 * i : 9 * i + 16, :] = g1[h, i].astype(F32)
        g2[h, me2[h]] = zg[h].astype(BF)
        for i in (1, 2, 3):
            g2_copy(h, i, me2[h]).start()

    def gather2(h):
        for i in (1, 2, 3):
            g2_copy(h, i, me2[h]).wait_send()
            g2_copy(h, i, (me2[h] + 4 - i) % 4).wait_recv()
        zf[h] = g2[h].astype(F32)
        rows = pl.ds(pl.multiple_of(128 * core + 32 * me1[h], 32), 32)
        for m in range(TILES):
            a = h * HALF + m * LANES
            wg[rows, a : a + LANES] = zf[h, :, 8 * m : 8 * m + 8, :].reshape(32, LANES).astype(BF)
        for i in (1, 2, 3):
            g3_copy(h, i, me1[h]).start()
        gc_copy(h, 0, core, me1[h]).start()

    def gather3(h, i):
        n = (me1[h] + 4 - i) % 4
        g3_copy(h, i, n).wait_recv()
        gc_copy(h, i, core, n).start()

    for c in feat_copies[0] + edge_copies:
        c.wait()
    basis(0)
    weight_rows(0)
    for c in feat_copies[1]:
        c.wait()
    basis(1)
    core_sum(0)
    weight_rows(1)
    core_sum(1)

    w_copy.wait()
    acc = dot(w[:, :256], bo[:256, :])
    for m in range(1, K):
        acc += dot(w[:, m * 256 : m * 256 + 256], bo[m * 256 : m * 256 + 256, :])
    out[...] = acc.astype(BF)

    def basis_grad(m, _):
        cols = pl.ds(pl.multiple_of(m * 256, 256), 256)
        g = dot(w[:, cols], cot[...], TN)
        big[0, cols, :] = g[:, :LANES]
        big[1, cols, :] = g[:, LANES:]
        return 0

    lax.fori_loop(0, K, basis_grad, 0)
    sum1(0)
    sum1(1)
    for k in range(K):
        for t in range(2):
            bgk[k, :, t * LANES : (t + 1) * LANES] = big[t, pl.ds(k, C, stride=K), :].astype(BF)
    sum2(0)
    sum2(1)

    def input_grad(dl):
        acc = dot(bgk[0], bmat[0, dl], NT)
        for k in range(1, K):
            acc += dot(bgk[k], bmat[k, dl], NT)
        return acc

    igp[0] = input_grad(0).astype(BF)
    igp[1] = input_grad(2).astype(BF)
    acc = dot(bhal[0], bgk[0], NT)
    for k in range(1, K):
        acc += dot(bhal[k], bgk[k], NT)
    for s in range(6):
        egs[s] = acc[s * 16 : s * 16 + 16].astype(BF)
    grad_copies = [
        remote(igp.at[0], gr.at[1], g_ss.at[0], g_rs.at[1], lat_peer(-1)),
        remote(igp.at[1], gr.at[0], g_ss.at[1], g_rs.at[0], lat_peer(1)),
    ] + [remote(egs.at[s], egr.at[s], h_ss.at[s], h_rs.at[s], edge_peer(s)) for s in range(6)]
    for c in grad_copies:
        c.start()
    sum3(0)
    sum3(1)
    gather1(0)
    gather1(1)
    gather2(0)
    gather2(1)

    for c in grad_copies:
        c.wait()
    edges = egr[0].astype(F32)
    for s in range(1, 6):
        edges += egr[s].astype(F32)
    acc = input_grad(1) + gr[0].astype(F32) + gr[1].astype(F32)
    edge_hi = edges.astype(BF)
    edge_lo = (edges - edge_hi.astype(F32)).astype(BF)
    acc += dot(edge_hi, sel, TN) + dot(edge_lo, sel, TN)
    ig[...] = acc.astype(BF)

    for i in (1, 3, 2):
        for h in range(2):
            gather3(h, i)
    for h in range(2):
        for i in range(4):
            gc_copy(h, i, core, (me1[h] + 4 - i) % 4).wait_send()
            gc_copy(h, i, 1 - core, (me1[h] + 4 - i) % 4).wait_recv()
        for i in (1, 2, 3):
            g3_copy(h, i, me1[h]).wait_send()


def per_device(features, weight, filter_table, row_range, basis_id, cotangent):
    vmem = pl.BlockSpec(memory_space=pltpu.VMEM)
    smem = pl.BlockSpec(memory_space=pltpu.SMEM)
    hbm = pl.BlockSpec(memory_space=pl.ANY)
    dma = pltpu.SemaphoreType.DMA
    scratch = [
        pltpu.VMEM((C, C * K), BF),
        pltpu.VMEM((2, C, 256), BF),
        pltpu.VMEM((16, C), BF),
        pltpu.VMEM((6, 16, C), BF),
        pltpu.VMEM((K, 3, 256, 256), BF),
        pltpu.VMEM((K, 96, 256), BF),
        pltpu.VMEM((2, C * K, LANES), F32),
        pltpu.VMEM((C * K, 256), BF),
        pltpu.VMEM((K, C, 256), BF),
        pltpu.VMEM((2, C, 256), BF),
        pltpu.VMEM((2, C, 256), BF),
        pltpu.VMEM((6, 16, C), BF),
        pltpu.VMEM((6, 16, C), BF),
        pltpu.VMEM((2, 128, HALF), BF),
        pltpu.VMEM((2, 128, HALF), BF),
        pltpu.VMEM((2, 128, HALF), F32),
        pltpu.VMEM((2, 128, HALF), BF),
        pltpu.VMEM((2, 4, 32, HALF), BF),
        pltpu.VMEM((2, 4, 80, LANES), F32),
        pltpu.VMEM((2, 4, 80, LANES), BF),
        pltpu.VMEM((2, 4, 80, LANES), BF),
        pltpu.VMEM((2, 80, LANES), F32),
        pltpu.VMEM((2, NZ, 16, LANES), BF),
        pltpu.VMEM((2, NZ, 16, LANES), BF),
        pltpu.VMEM((2, NZ, 16, LANES), BF),
        pltpu.VMEM((2, 4, 80, LANES), BF),
        dma,
        dma((2, 2)), dma((2, 2)), dma((6,)), dma((6,)), dma((2,)), dma((2,)), dma((6,)), dma((6,)),
        dma((2,)), dma((2,)),
        dma((2, 4)), dma((2, 4)), dma((2, 4)), dma((2, 4)), dma((2, NZ)), dma((2, NZ)),
        dma((2, NZ)), dma((2, NZ)), dma((2, 4)), dma((2, 4)), dma((2, 4)), dma((2, 4)),
        dma((2, 4)), dma((2, 4)),
    ]
    out, ig, wg = pl.pallas_call(
        kernel,
        out_shape=(
            jax.ShapeDtypeStruct((C, 256), BF),
            jax.ShapeDtypeStruct((C, 256), BF),
            jax.ShapeDtypeStruct((C, C * K), BF),
        ),
        in_specs=[vmem, vmem, hbm, smem, smem, smem],
        out_specs=(vmem, vmem, vmem),
        scratch_shapes=scratch,
        compiler_params=pltpu.CompilerParams(
            collective_id=0, has_side_effects=True, vmem_limit_bytes=48 * 1024 * 1024
        ),
    )(
        features.reshape(C, 256),
        cotangent.reshape(C, 256),
        weight,
        filter_table.transpose(1, 2, 0),
        row_range.T,
        basis_id.T,
    )
    return out.reshape(C, 2, LANES), ig.reshape(C, 2, LANES), wg.astype(F32)


def solution(mesh):
    in_specs = (P(None, "lat", "lon"), P(), P(), P(), P(), P(None, "lat", "lon"))
    out_specs = (P(None, "lat", "lon"), P(None, "lat", "lon"), P())
    return jax.shard_map(
        per_device, mesh=mesh, in_specs=in_specs, out_specs=out_specs, check_vma=False
    )
```

```python
import functools
import math

import jax
import jax.numpy as jnp
from jax import lax
from jax.experimental import pallas as pl
from jax.experimental.pallas import tpu as pltpu
from jax.sharding import PartitionSpec as P

BF = jnp.bfloat16
F32 = jnp.float32
MESH = pl.DeviceIdType.MESH
C = 256
K = 9
LANES = 128
NZ = 8
N_LAT, N_LON = 64, 4
N_ROWS = 128
HALF = C * K // 2
TILES = HALF // LANES
NT = (((1,), (1,)), ((), ()))
TN = (((0,), (0,)), ((), ()))
NN = (((1,), (0,)), ((), ()))


def dot(a, b, dims=NN):
    return lax.dot_general(a, b, dims, preferred_element_type=F32)


def kernel(
    feat_hbm, cot_hbm, w_hbm, table_hbm, rng_hbm, ids_hbm,
    out, ig, wg,
    raw, feat, cot, table, rng, ids, w, fx, e_send, e_recv, bmat, bhal, big, bo, bgk, igp, gr, egs, egr,
    cs, cr, own, s1, r1, zf, s2, r2, zg, s3, r3, g1, g2,
    in_sem, f_ss, f_rs, e_ss, e_rs, g_ss, g_rs, h_ss, h_rs, c_ss, c_rs,
    s1_ss, s1_rs, s2_ss, s2_rs, s3_ss, s3_rs,
    g1_ss, g1_rs, g2_ss, g2_rs, g3_ss, g3_rs, gc_ss, gc_rs,
):
    la, lo = lax.axis_index("lat"), lax.axis_index("lon")
    y, z, xh = la // 16, (la // 2) % 8, la % 2
    xl, core = lo // 2, lo % 2
    x = xh * 2 + xl
    sibling = (la, lo + 1 - 2 * core)
    me1, me2 = (y, x), (x, y)

    def lat_peer(dl):
        return (lax.rem(la + dl + N_LAT, N_LAT), lo)

    def edge_peer(s):
        dl, dc = s // 2 - 1, 2 * (s % 2) - 1
        return (lax.rem(la + dl + N_LAT, N_LAT), lax.rem(lo + dc + N_LON, N_LON))

    def y_peer(i):
        return ((((y + i) % 4) * 8 + z) * 2 + xh, lo)

    def x_peer(i):
        px = (x + i) % 4
        return ((y * 8 + z) * 2 + px // 2, (px % 2) * 2 + core)

    def z_peer(i):
        return ((y * 8 + (z + i) % 8) * 2 + xh, lo)

    peer1, peer2 = (y_peer, x_peer), (x_peer, y_peer)

    in_copies = [
        pltpu.make_async_copy(src, dst, in_sem.at[i])
        for i, (src, dst) in enumerate(
            [
                (feat_hbm, raw.at[0]),
                (table_hbm, table),
                (rng_hbm, rng),
                (ids_hbm, ids),
                (cot_hbm, raw.at[1]),
                (w_hbm, w),
            ]
        )
    ]
    for c in in_copies:
        c.start()

    barrier = pltpu.get_barrier_semaphore()
    peers = [lat_peer(-1), lat_peer(1)] + [edge_peer(s) for s in range(6)]
    peers += [y_peer(i) for i in (1, 2, 3)] + [x_peer(i) for i in (1, 3)]
    peers += [z_peer(i) for i in range(1, NZ)]
    for peer in peers:
        pl.semaphore_signal(barrier, inc=1, device_id=peer, device_id_type=MESH)

    def rows_to_lanes(ref, dst):
        v = ref[...].astype(F32)
        dst[:, :LANES] = v[:, 0, :].astype(BF)
        dst[:, LANES:] = v[:, 1, :].astype(BF)

    def lanes_to_rows(v):
        return jnp.stack([v[:, :LANES], v[:, LANES:]], axis=1).astype(BF)

    in_copies[0].wait()
    rows_to_lanes(raw.at[0], feat)

    rho = lax.broadcasted_iota(jnp.int32, (16, 2 * LANES), 0)
    col = lax.broadcasted_iota(jnp.int32, (16, 2 * LANES), 1)
    edge_i = rho % 4
    edge_col = jnp.where(edge_i < 2, edge_i, edge_i + LANES - 4)
    sel = ((rho < 8) & (col == (rho // 4) * LANES + edge_col)).astype(F32).astype(BF)
    e_send[...] = dot(sel, feat[...], NT).astype(BF)

    pl.semaphore_wait(barrier, len(peers))

    def remote(src, dst, ss, rs, peer):
        return pltpu.make_async_remote_copy(
            src_ref=src, dst_ref=dst, send_sem=ss, recv_sem=rs, device_id=peer, device_id_type=MESH
        )

    half_rows = [slice(0, 128), slice(128, 256)]
    feat_copies = [
        [
            remote(
                feat.at[half_rows[h]], fx.at[1, half_rows[h]], f_ss.at[h, 0], f_rs.at[h, 1], lat_peer(-1)
            ),
            remote(
                feat.at[half_rows[h]], fx.at[0, half_rows[h]], f_ss.at[h, 1], f_rs.at[h, 0], lat_peer(1)
            ),
        ]
        for h in range(2)
    ]
    edge_copies = [
        remote(e_send, e_recv.at[5 - s], e_ss.at[s], e_rs.at[5 - s], edge_peer(s)) for s in range(6)
    ]
    for c in feat_copies[0] + edge_copies + feat_copies[1]:
        c.start()

    for c in in_copies[1:4]:
        c.wait()
    diag = lax.broadcasted_iota(jnp.int32, (LANES, LANES), 0) - lax.broadcasted_iota(
        jnp.int32, (LANES, LANES), 1
    ) + 2
    hr = lax.broadcasted_iota(jnp.int32, (16, LANES), 0)
    hp = lax.broadcasted_iota(jnp.int32, (16, LANES), 1)
    row_ids, row_act = [], []
    for t in range(2):
        g = la * 2 + t
        r0, r1_ = rng[0, g], rng[1, g]
        row_ids.append([ids[j, g] for j in range(5)])
        row_act.append(
            [
                (j >= r0) & (j < r1_) & (g + j - 2 >= 0) & (g + j - 2 < N_ROWS)
                for j in range(5)
            ]
        )
    zero_block = jnp.zeros((LANES, LANES), BF)

    def build(k, _):
        coef = [
            [
                [jnp.where(row_act[t][j], table[k, l, row_ids[t][j]], 0.0) for l in range(5)]
                for j in range(5)
            ]
            for t in range(2)
        ]
        for t in range(2):
            lanes = slice(t * LANES, (t + 1) * LANES)
            for e in range(6):
                j = e - t
                rows = slice((e % 2) * LANES, (e % 2 + 1) * LANES)
                if j < 0 or j > 4:
                    bmat[k, e // 2, rows, lanes] = zero_block
                    continue
                v = jnp.zeros((LANES, LANES), F32)
                for l in range(5):
                    v = jnp.where(diag == l, coef[t][j][l], v)
                bmat[k, e // 2, rows, lanes] = v.astype(BF)
            for s in range(6):
                v = jnp.zeros((16, LANES), F32)
                for r in range(2):
                    j = (s // 2) * 2 + r - t
                    if j < 0 or j > 4:
                        continue
                    if s % 2 == 0:
                        outer = (hr == r * 4 + 2) & (hp == 0) | (hr == r * 4 + 3) & (hp == 1)
                        inner = (hr == r * 4 + 3) & (hp == 0)
                        v = jnp.where(outer, coef[t][j][0], jnp.where(inner, coef[t][j][1], v))
                    else:
                        outer = (hr == r * 4) & (hp == 126) | (hr == r * 4 + 1) & (hp == 127)
                        inner = (hr == r * 4) & (hp == 127)
                        v = jnp.where(outer, coef[t][j][4], jnp.where(inner, coef[t][j][3], v))
                bhal[k, s * 16 : s * 16 + 16, lanes] = v.astype(BF)
        return 0

    lax.fori_loop(0, K, build, 0)
    for h in range(2):
        zf[h, :, 72:80, :] = jnp.zeros((4, 8, LANES), F32)

    in_copies[4].wait()
    rows_to_lanes(raw.at[1], cot)

    theirs = pl.ds(pl.multiple_of(128 * (1 - core), 128), 128)
    mine = pl.ds(pl.multiple_of(128 * core, 128), 128)
    chunks = [(0, 256), (256, 512), (512, 768), (768, 1024), (1024, 1152)]

    def core_copy(h):
        return remote(cs.at[h], cr.at[h], c_ss.at[h], c_rs.at[h], sibling)

    def basis(h):
        hc = half_rows[h]
        halo = e_recv[:, :, hc].reshape(96, 128)
        for k in range(K):
            acc = dot(feat[hc, :], bmat[k, 1]) + dot(fx[0, hc, :], bmat[k, 0])
            acc += dot(fx[1, hc, :], bmat[k, 2]) + dot(halo, bhal[k], TN)
            rows = pl.ds(h * HALF + k, 128, stride=K)
            big[0, rows, :] = acc[:, :LANES]
            big[1, rows, :] = acc[:, LANES:]
        for a, b in chunks:
            rows = slice(h * HALF + a, h * HALF + b)
            bo[rows, :LANES] = big[0, rows, :].astype(BF)
            bo[rows, LANES:] = big[1, rows, :].astype(BF)
            cs[h, :, a:b] = dot(cot[theirs, :], bo[rows, :], NT).astype(BF)
        core_copy(h).start()

    def weight_rows(h):
        for a, b in chunks:
            own[h, :, a:b] = dot(cot[mine, :], bo[h * HALF + a : h * HALF + b, :], NT)

    def s1_copy(h, i):
        rows = pl.ds(pl.multiple_of(32 * ((me1[h] + i) % 4), 32), 32)
        return remote(s1.at[h, rows], r1.at[h, i], s1_ss.at[h, i], s1_rs.at[h, i], peer1[h](i))

    def s2_copy(h, i):
        n = (me2[h] + i) % 4
        return remote(s2.at[h, n], r2.at[h, i], s2_ss.at[h, i], s2_rs.at[h, i], peer2[h](i))

    def s3_copy(h, i):
        n = (z + i) % 8
        return remote(s3.at[h, n], r3.at[h, i], s3_ss.at[h, i], s3_rs.at[h, i], z_peer(i))

    def g1_copy(h, i, n):
        return remote(g1.at[h, n], g1.at[h, n], g1_ss.at[h, i], g1_rs.at[h, i], z_peer(i))

    def g2_copy(h, i, n):
        return remote(g2.at[h, n], g2.at[h, n], g2_ss.at[h, i], g2_rs.at[h, i], peer2[h](i))

    def piece(h, c, n):
        rows = pl.ds(pl.multiple_of(128 * c + 32 * n, 32), 32)
        return wg.at[rows, h * HALF : (h + 1) * HALF]

    def g3_copy(h, i, n):
        ref = piece(h, core, n)
        return remote(ref, ref, g3_ss.at[h, i], g3_rs.at[h, i], peer1[h](i))

    def gc_copy(h, i, c, n):
        ref = piece(h, c, n)
        return remote(ref, ref, gc_ss.at[h, i], gc_rs.at[h, i], sibling)

    def core_sum(h):
        core_copy(h).wait()
        s1[h] = (own[h] + cr[h].astype(F32)).astype(BF)
        for i in (1, 2, 3):
            s1_copy(h, i).start()

    def sum1(h):
        rows = pl.ds(pl.multiple_of(32 * me1[h], 32), 32)
        total = s1[h, rows, :].astype(F32)
        for i in (1, 2, 3):
            s1_copy(h, i).wait()
            total += r1[h, i].astype(F32)
        for m in range(TILES):
            tile = total[:, m * LANES : (m + 1) * LANES]
            zf[h, :, 8 * m : 8 * m + 8, :] = tile.reshape(4, 8, LANES)
        s2[h] = zf[h].astype(BF)
        for i in (1, 2, 3):
            s2_copy(h, i).start()

    def sum2(h):
        total = s2[h, me2[h]].astype(F32)
        for i in (1, 2, 3):
            s2_copy(h, i).wait()
            total += r2[h, i].astype(F32)
        zg[h] = total
        for i in range(NZ):
            s3[h, i] = zg[h, 9 * i : 9 * i + 16, :].astype(BF)
        for i in range(1, NZ):
            s3_copy(h, i).start()

    def sum3(h):
        total = s3[h, z].astype(F32)
        for i in range(1, NZ):
            s3_copy(h, i).wait()
            total += r3[h, i].astype(F32)
        g1[h, z] = (total * F32(1.0 / math.sqrt(N_ROWS * N_LON * LANES))).astype(BF)
        for i in range(1, NZ):
            g1_copy(h, i, z).start()

    def gather1(h):
        for i in range(1, NZ):
            g1_copy(h, i, z).wait_send()
            g1_copy(h, i, (z + 8 - i) % 8).wait_recv()
        for i in range(NZ):
            zg[h, 9 * i : 9 * i + 16, :] = g1[h, i].astype(F32)
        g2[h, me2[h]] = zg[h].astype(BF)
        for i in (1, 2, 3):
            g2_copy(h, i, me2[h]).start()

    def gather2(h):
        for i in (1, 2, 3):
            g2_copy(h, i, me2[h]).wait_send()
            g2_copy(h, i, (me2[h] + 4 - i) % 4).wait_recv()
        zf[h] = g2[h].astype(F32)
        rows = pl.ds(pl.multiple_of(128 * core + 32 * me1[h], 32), 32)
        for m in range(TILES):
            a = h * HALF + m * LANES
            wg[rows, a : a + LANES] = zf[h, :, 8 * m : 8 * m + 8, :].reshape(32, LANES).astype(BF)
        for i in (1, 2, 3):
            g3_copy(h, i, me1[h]).start()
        gc_copy(h, 0, core, me1[h]).start()

    def gather3(h, i):
        n = (me1[h] + 4 - i) % 4
        g3_copy(h, i, n).wait_recv()
        gc_copy(h, i, core, n).start()

    for c in feat_copies[0] + edge_copies:
        c.wait()
    basis(0)
    weight_rows(0)
    for c in feat_copies[1]:
        c.wait()
    basis(1)
    core_sum(0)
    weight_rows(1)
    core_sum(1)

    in_copies[5].wait()
    acc = dot(w[:, :256], bo[:256, :])
    for m in range(1, K):
        acc += dot(w[:, m * 256 : m * 256 + 256], bo[m * 256 : m * 256 + 256, :])
    out[...] = lanes_to_rows(acc)

    def basis_grad(m, _):
        cols = pl.ds(pl.multiple_of(m * 256, 256), 256)
        g = dot(w[:, cols], cot[...], TN)
        big[0, cols, :] = g[:, :LANES]
        big[1, cols, :] = g[:, LANES:]
        return 0

    lax.fori_loop(0, K, basis_grad, 0)
    sum1(0)
    sum1(1)
    for k in range(K):
        for t in range(2):
            bgk[k, :, t * LANES : (t + 1) * LANES] = big[t, pl.ds(k, C, stride=K), :].astype(BF)
    sum2(0)
    sum2(1)

    def input_grad(dl):
        acc = dot(bgk[0], bmat[0, dl], NT)
        for k in range(1, K):
            acc += dot(bgk[k], bmat[k, dl], NT)
        return acc

    igp[0] = input_grad(0).astype(BF)
    igp[1] = input_grad(2).astype(BF)
    acc = dot(bhal[0], bgk[0], NT)
    for k in range(1, K):
        acc += dot(bhal[k], bgk[k], NT)
    for s in range(6):
        egs[s] = acc[s * 16 : s * 16 + 16].astype(BF)
    grad_copies = [
        remote(igp.at[0], gr.at[1], g_ss.at[0], g_rs.at[1], lat_peer(-1)),
        remote(igp.at[1], gr.at[0], g_ss.at[1], g_rs.at[0], lat_peer(1)),
    ] + [remote(egs.at[s], egr.at[s], h_ss.at[s], h_rs.at[s], edge_peer(s)) for s in range(6)]
    for c in grad_copies:
        c.start()
    sum3(0)
    sum3(1)
    gather1(0)
    gather1(1)
    gather2(0)
    gather2(1)

    for c in grad_copies:
        c.wait()
    edges = egr[0].astype(F32)
    for s in range(1, 6):
        edges += egr[s].astype(F32)
    acc = input_grad(1) + gr[0].astype(F32) + gr[1].astype(F32)
    edge_hi = edges.astype(BF)
    edge_lo = (edges - edge_hi.astype(F32)).astype(BF)
    acc += dot(edge_hi, sel, TN) + dot(edge_lo, sel, TN)
    ig[...] = lanes_to_rows(acc)

    for i in (1, 3, 2):
        for h in range(2):
            gather3(h, i)
    for h in range(2):
        for i in range(4):
            gc_copy(h, i, core, (me1[h] + 4 - i) % 4).wait_send()
            gc_copy(h, i, 1 - core, (me1[h] + 4 - i) % 4).wait_recv()
        for i in (1, 2, 3):
            g3_copy(h, i, me1[h]).wait_send()


def per_device(features, weight, filter_table, row_range, basis_id, cotangent):
    vmem = pl.BlockSpec(memory_space=pltpu.VMEM)
    hbm = pl.BlockSpec(memory_space=pltpu.HBM)
    dma = pltpu.SemaphoreType.DMA
    scratch = [
        pltpu.VMEM((2, C, 2, LANES), BF),
        pltpu.VMEM((C, 256), BF),
        pltpu.VMEM((C, 256), BF),
        pltpu.SMEM((K, 5, 16), F32),
        pltpu.SMEM((2, N_ROWS), jnp.int32),
        pltpu.SMEM((5, N_ROWS), jnp.int32),
        pltpu.VMEM((C, C * K), BF),
        pltpu.VMEM((2, C, 256), BF),
        pltpu.VMEM((16, C), BF),
        pltpu.VMEM((6, 16, C), BF),
        pltpu.VMEM((K, 3, 256, 256), BF),
        pltpu.VMEM((K, 96, 256), BF),
        pltpu.VMEM((2, C * K, LANES), F32),
        pltpu.VMEM((C * K, 256), BF),
        pltpu.VMEM((K, C, 256), BF),
        pltpu.VMEM((2, C, 256), BF),
        pltpu.VMEM((2, C, 256), BF),
        pltpu.VMEM((6, 16, C), BF),
        pltpu.VMEM((6, 16, C), BF),
        pltpu.VMEM((2, 128, HALF), BF),
        pltpu.VMEM((2, 128, HALF), BF),
        pltpu.VMEM((2, 128, HALF), F32),
        pltpu.VMEM((2, 128, HALF), BF),
        pltpu.VMEM((2, 4, 32, HALF), BF),
        pltpu.VMEM((2, 4, 80, LANES), F32),
        pltpu.VMEM((2, 4, 80, LANES), BF),
        pltpu.VMEM((2, 4, 80, LANES), BF),
        pltpu.VMEM((2, 80, LANES), F32),
        pltpu.VMEM((2, NZ, 16, LANES), BF),
        pltpu.VMEM((2, NZ, 16, LANES), BF),
        pltpu.VMEM((2, NZ, 16, LANES), BF),
        pltpu.VMEM((2, 4, 80, LANES), BF),
        dma((6,)),
        dma((2, 2)), dma((2, 2)), dma((6,)), dma((6,)), dma((2,)), dma((2,)), dma((6,)), dma((6,)),
        dma((2,)), dma((2,)),
        dma((2, 4)), dma((2, 4)), dma((2, 4)), dma((2, 4)), dma((2, NZ)), dma((2, NZ)),
        dma((2, NZ)), dma((2, NZ)), dma((2, 4)), dma((2, 4)), dma((2, 4)), dma((2, 4)),
        dma((2, 4)), dma((2, 4)),
    ]
    out, ig, wg = pl.pallas_call(
        kernel,
        out_shape=(
            pltpu.VMEM((C, 2, LANES), BF),
            pltpu.VMEM((C, 2, LANES), BF),
            pltpu.VMEM((C, C * K), BF),
        ),
        in_specs=[hbm] * 6,
        out_specs=(vmem, vmem, vmem),
        scratch_shapes=scratch,
        compiler_params=pltpu.CompilerParams(
            collective_id=0, has_side_effects=True, vmem_limit_bytes=56 * 1024 * 1024
        ),
    )(
        features,
        cotangent,
        weight,
        filter_table.transpose(1, 2, 0),
        row_range.T,
        basis_id.T,
    )
    return out, ig, wg.astype(F32)


def solution(mesh):
    in_specs = (P(None, "lat", "lon"), P(), P(), P(), P(), P(None, "lat", "lon"))
    out_specs = (P(None, "lat", "lon"), P(None, "lat", "lon"), P())
    return jax.shard_map(
        per_device, mesh=mesh, in_specs=in_specs, out_specs=out_specs, check_vma=False
    )
```

```python
import functools
import math

import jax
import jax.numpy as jnp
from jax import lax
from jax.experimental import pallas as pl
from jax.experimental.pallas import tpu as pltpu
from jax.sharding import PartitionSpec as P

BF = jnp.bfloat16
F32 = jnp.float32
MESH = pl.DeviceIdType.MESH
C = 256
K = 9
LANES = 128
NZ = 8
N_LAT, N_LON = 64, 4
N_ROWS = 128
HALF = C * K // 2
TILES = HALF // LANES
NT = (((1,), (1,)), ((), ()))
TN = (((0,), (0,)), ((), ()))
NN = (((1,), (0,)), ((), ()))


def dot(a, b, dims=NN):
    return lax.dot_general(a, b, dims, preferred_element_type=F32)


def kernel(
    feat_hbm, cot_hbm, w_hbm, table_hbm, rng_hbm, ids_hbm,
    out, ig, wg,
    raw, feat, cot, table, rng, ids, w, fx, e_send, e_recv, bmat, bhal, big, bo, bgk, igp, gr, egs, egr,
    cs, cr, own, s1, r1, zf, s2, r2, zr, g2, wb, igo,
    in_sem, f_ss, f_rs, e_ss, e_rs, g_ss, g_rs, h_ss, h_rs, c_ss, c_rs,
    s1_ss, s1_rs, s2_ss, s2_rs, z_ss, z_rs,
    g2_ss, g2_rs, g3_ss, g3_rs, gc_ss, gc_rs,
):
    la, lo = lax.axis_index("lat"), lax.axis_index("lon")
    y, z, xh = la // 16, (la // 2) % 8, la % 2
    xl, core = lo // 2, lo % 2
    x = xh * 2 + xl
    sibling = (la, lo + 1 - 2 * core)
    me1, me2 = (y, x), (x, y)

    def lat_peer(dl):
        return (lax.rem(la + dl + N_LAT, N_LAT), lo)

    def edge_peer(s):
        dl, dc = s // 2 - 1, 2 * (s % 2) - 1
        return (lax.rem(la + dl + N_LAT, N_LAT), lax.rem(lo + dc + N_LON, N_LON))

    def y_peer(i):
        return ((((y + i) % 4) * 8 + z) * 2 + xh, lo)

    def x_peer(i):
        px = (x + i) % 4
        return ((y * 8 + z) * 2 + px // 2, (px % 2) * 2 + core)

    def z_peer(i):
        return ((y * 8 + (z + i) % 8) * 2 + xh, lo)

    peer1, peer2 = (y_peer, x_peer), (x_peer, y_peer)

    in_copies = [
        pltpu.make_async_copy(src, dst, in_sem.at[i])
        for i, (src, dst) in enumerate(
            [
                (feat_hbm, raw.at[0]),
                (table_hbm, table),
                (rng_hbm, rng),
                (ids_hbm, ids),
                (cot_hbm, raw.at[1]),
                (w_hbm, w),
            ]
        )
    ]
    for c in in_copies:
        c.start()

    barrier = pltpu.get_barrier_semaphore()
    peers = [lat_peer(-1), lat_peer(1)] + [edge_peer(s) for s in range(6)]
    peers += [y_peer(i) for i in (1, 2, 3)] + [x_peer(i) for i in (1, 3)]
    peers += [z_peer(i) for i in range(1, NZ)]
    for peer in peers:
        pl.semaphore_signal(barrier, inc=1, device_id=peer, device_id_type=MESH)

    def rows_to_lanes(ref, dst):
        v = ref[...].astype(F32)
        dst[:, :LANES] = v[:, 0, :].astype(BF)
        dst[:, LANES:] = v[:, 1, :].astype(BF)

    def lanes_to_rows(v):
        return jnp.stack([v[:, :LANES], v[:, LANES:]], axis=1).astype(BF)

    in_copies[0].wait()
    rows_to_lanes(raw.at[0], feat)

    rho = lax.broadcasted_iota(jnp.int32, (16, 2 * LANES), 0)
    col = lax.broadcasted_iota(jnp.int32, (16, 2 * LANES), 1)
    edge_i = rho % 4
    edge_col = jnp.where(edge_i < 2, edge_i, edge_i + LANES - 4)
    sel = ((rho < 8) & (col == (rho // 4) * LANES + edge_col)).astype(F32).astype(BF)
    e_send[...] = dot(sel, feat[...], NT).astype(BF)

    pl.semaphore_wait(barrier, len(peers))

    def remote(src, dst, ss, rs, peer):
        return pltpu.make_async_remote_copy(
            src_ref=src, dst_ref=dst, send_sem=ss, recv_sem=rs, device_id=peer, device_id_type=MESH
        )

    half_rows = [slice(0, 128), slice(128, 256)]
    feat_copies = [
        [
            remote(
                feat.at[half_rows[h]], fx.at[1, half_rows[h]], f_ss.at[h, 0], f_rs.at[h, 1], lat_peer(-1)
            ),
            remote(
                feat.at[half_rows[h]], fx.at[0, half_rows[h]], f_ss.at[h, 1], f_rs.at[h, 0], lat_peer(1)
            ),
        ]
        for h in range(2)
    ]
    edge_copies = [
        remote(e_send, e_recv.at[5 - s], e_ss.at[s], e_rs.at[5 - s], edge_peer(s)) for s in range(6)
    ]
    for c in feat_copies[0] + edge_copies + feat_copies[1]:
        c.start()

    for c in in_copies[1:4]:
        c.wait()
    diag = lax.broadcasted_iota(jnp.int32, (LANES, LANES), 0) - lax.broadcasted_iota(
        jnp.int32, (LANES, LANES), 1
    ) + 2
    hr = lax.broadcasted_iota(jnp.int32, (16, LANES), 0)
    hp = lax.broadcasted_iota(jnp.int32, (16, LANES), 1)
    row_ids, row_act = [], []
    for t in range(2):
        g = la * 2 + t
        r0, r1_ = rng[0, g], rng[1, g]
        row_ids.append([ids[j, g] for j in range(5)])
        row_act.append(
            [
                (j >= r0) & (j < r1_) & (g + j - 2 >= 0) & (g + j - 2 < N_ROWS)
                for j in range(5)
            ]
        )
    zero_block = jnp.zeros((LANES, LANES), BF)

    def build(k, _):
        coef = [
            [
                [jnp.where(row_act[t][j], table[k, l, row_ids[t][j]], 0.0) for l in range(5)]
                for j in range(5)
            ]
            for t in range(2)
        ]
        for t in range(2):
            lanes = slice(t * LANES, (t + 1) * LANES)
            for e in range(6):
                j = e - t
                rows = slice((e % 2) * LANES, (e % 2 + 1) * LANES)
                if j < 0 or j > 4:
                    bmat[k, e // 2, rows, lanes] = zero_block
                    continue
                v = jnp.zeros((LANES, LANES), F32)
                for l in range(5):
                    v = jnp.where(diag == l, coef[t][j][l], v)
                bmat[k, e // 2, rows, lanes] = v.astype(BF)
            for s in range(6):
                v = jnp.zeros((16, LANES), F32)
                for r in range(2):
                    j = (s // 2) * 2 + r - t
                    if j < 0 or j > 4:
                        continue
                    if s % 2 == 0:
                        outer = (hr == r * 4 + 2) & (hp == 0) | (hr == r * 4 + 3) & (hp == 1)
                        inner = (hr == r * 4 + 3) & (hp == 0)
                        v = jnp.where(outer, coef[t][j][0], jnp.where(inner, coef[t][j][1], v))
                    else:
                        outer = (hr == r * 4) & (hp == 126) | (hr == r * 4 + 1) & (hp == 127)
                        inner = (hr == r * 4) & (hp == 127)
                        v = jnp.where(outer, coef[t][j][4], jnp.where(inner, coef[t][j][3], v))
                bhal[k, s * 16 : s * 16 + 16, lanes] = v.astype(BF)
        return 0

    lax.fori_loop(0, K, build, 0)
    for h in range(2):
        zf[h, :, 72:80, :] = jnp.zeros((4, 8, LANES), F32)

    in_copies[4].wait()
    rows_to_lanes(raw.at[1], cot)

    theirs = pl.ds(pl.multiple_of(128 * (1 - core), 128), 128)
    mine = pl.ds(pl.multiple_of(128 * core, 128), 128)
    chunks = [(0, 256), (256, 512), (512, 768), (768, 1024), (1024, 1152)]

    def core_copy(h):
        return remote(cs.at[h], cr.at[h], c_ss.at[h], c_rs.at[h], sibling)

    def basis(h):
        hc = half_rows[h]
        halo = e_recv[:, :, hc].reshape(96, 128)
        for k in range(K):
            acc = dot(feat[hc, :], bmat[k, 1]) + dot(fx[0, hc, :], bmat[k, 0])
            acc += dot(fx[1, hc, :], bmat[k, 2]) + dot(halo, bhal[k], TN)
            rows = pl.ds(h * HALF + k, 128, stride=K)
            big[0, rows, :] = acc[:, :LANES]
            big[1, rows, :] = acc[:, LANES:]
        for a, b in chunks:
            rows = slice(h * HALF + a, h * HALF + b)
            bo[rows, :LANES] = big[0, rows, :].astype(BF)
            bo[rows, LANES:] = big[1, rows, :].astype(BF)
            cs[h, :, a:b] = dot(cot[theirs, :], bo[rows, :], NT).astype(BF)
        core_copy(h).start()

    def weight_rows(h):
        for a, b in chunks:
            own[h, :, a:b] = dot(cot[mine, :], bo[h * HALF + a : h * HALF + b, :], NT)

    def s1_copy(h, i):
        rows = pl.ds(pl.multiple_of(32 * ((me1[h] + i) % 4), 32), 32)
        return remote(s1.at[h, rows], r1.at[h, i], s1_ss.at[h, i], s1_rs.at[h, i], peer1[h](i))

    def s2_copy(h, i):
        n = (me2[h] + i) % 4
        return remote(s2.at[h, n], r2.at[h, i], s2_ss.at[h, i], s2_rs.at[h, i], peer2[h](i))

    def z_copy(h, i, n):
        return remote(zr.at[h, n], zr.at[h, n], z_ss.at[h, i], z_rs.at[h, i], z_peer(i))

    def g2_copy(h, i, n):
        return remote(g2.at[h, n], g2.at[h, n], g2_ss.at[h, i], g2_rs.at[h, i], peer2[h](i))

    def piece(h, c, n):
        rows = pl.ds(pl.multiple_of(128 * c + 32 * n, 32), 32)
        return wb.at[rows, h * HALF : (h + 1) * HALF]

    def g3_copy(h, i, n):
        ref = piece(h, core, n)
        return remote(ref, ref, g3_ss.at[h, i], g3_rs.at[h, i], peer1[h](i))

    def gc_copy(h, i, c, n):
        ref = piece(h, c, n)
        return remote(ref, ref, gc_ss.at[h, i], gc_rs.at[h, i], sibling)

    def core_sum(h):
        core_copy(h).wait()
        s1[h] = (own[h] + cr[h].astype(F32)).astype(BF)
        for i in (1, 2, 3):
            s1_copy(h, i).start()

    def sum1(h):
        rows = pl.ds(pl.multiple_of(32 * me1[h], 32), 32)
        total = s1[h, rows, :].astype(F32)
        for i in (1, 2, 3):
            s1_copy(h, i).wait()
            total += r1[h, i].astype(F32)
        for m in range(TILES):
            tile = total[:, m * LANES : (m + 1) * LANES]
            zf[h, :, 8 * m : 8 * m + 8, :] = tile.reshape(4, 8, LANES)
        s2[h] = zf[h].astype(BF)
        for i in (1, 2, 3):
            s2_copy(h, i).start()

    def sum2(h):
        total = s2[h, me2[h]].astype(F32)
        for i in (1, 2, 3):
            s2_copy(h, i).wait()
            total += r2[h, i].astype(F32)
        zr[h, z] = total.astype(BF)
        for i in (4, 3, 5, 2, 6, 1, 7):
            z_copy(h, i, z).start()

    def sum_z(h):
        for i in range(1, NZ):
            z_copy(h, i, z).wait_send()
            z_copy(h, i, (z + 8 - i) % 8).wait_recv()
        total = zr[h, 0].astype(F32)
        for i in range(1, NZ):
            total += zr[h, i].astype(F32)
        total *= F32(1.0 / math.sqrt(N_ROWS * N_LON * LANES))
        g2[h, me2[h]] = total.astype(BF)
        for i in (2, 1, 3):
            g2_copy(h, i, me2[h]).start()

    def gather2(h):
        for i in (1, 2, 3):
            g2_copy(h, i, me2[h]).wait_send()
            g2_copy(h, i, (me2[h] + 4 - i) % 4).wait_recv()
        zf[h] = g2[h].astype(F32)
        rows = pl.ds(pl.multiple_of(128 * core + 32 * me1[h], 32), 32)
        for m in range(TILES):
            a = h * HALF + m * LANES
            wb[rows, a : a + LANES] = zf[h, :, 8 * m : 8 * m + 8, :].reshape(32, LANES).astype(BF)
        for i in (2, 1, 3):
            g3_copy(h, i, me1[h]).start()
        gc_copy(h, 0, core, me1[h]).start()
        widen(h, core, me1[h])

    def widen(h, c, n):
        rows = pl.ds(pl.multiple_of(128 * c + 32 * n, 32), 32)
        cols = slice(h * HALF, (h + 1) * HALF)
        wg[rows, cols] = wb[rows, cols].astype(F32)

    def gather3(h, i):
        n = (me1[h] + 4 - i) % 4
        g3_copy(h, i, n).wait_recv()
        gc_copy(h, i, core, n).start()
        widen(h, core, n)

    def gather_core(h, i):
        n = (me1[h] + 4 - i) % 4
        gc_copy(h, i, 1 - core, n).wait_recv()
        widen(h, 1 - core, n)

    for c in feat_copies[0] + edge_copies:
        c.wait()
    basis(0)
    weight_rows(0)
    core_sum(0)
    for c in feat_copies[1]:
        c.wait()
    basis(1)
    weight_rows(1)
    core_sum(1)

    in_copies[5].wait()
    acc = dot(w[:, :256], bo[:256, :])
    for m in range(1, K):
        acc += dot(w[:, m * 256 : m * 256 + 256], bo[m * 256 : m * 256 + 256, :])
    out[...] = lanes_to_rows(acc)
    sum1(0)

    def basis_grad(m, _):
        cols = pl.ds(pl.multiple_of(m * 256, 256), 256)
        g = dot(w[:, cols], cot[...], TN)
        big[0, cols, :] = g[:, :LANES]
        big[1, cols, :] = g[:, LANES:]
        return 0

    lax.fori_loop(0, K, basis_grad, 0)
    sum1(1)
    for k in range(K):
        for t in range(2):
            bgk[k, :, t * LANES : (t + 1) * LANES] = big[t, pl.ds(k, C, stride=K), :].astype(BF)
    sum2(0)

    def input_grad(dl):
        acc = dot(bgk[0], bmat[0, dl], NT)
        for k in range(1, K):
            acc += dot(bgk[k], bmat[k, dl], NT)
        return acc

    igp[0] = input_grad(0).astype(BF)
    sum2(1)
    igp[1] = input_grad(2).astype(BF)
    acc = dot(bhal[0], bgk[0], NT)
    for k in range(1, K):
        acc += dot(bhal[k], bgk[k], NT)
    for s in range(6):
        egs[s] = acc[s * 16 : s * 16 + 16].astype(BF)
    grad_copies = [
        remote(igp.at[0], gr.at[1], g_ss.at[0], g_rs.at[1], lat_peer(-1)),
        remote(igp.at[1], gr.at[0], g_ss.at[1], g_rs.at[0], lat_peer(1)),
    ] + [remote(egs.at[s], egr.at[s], h_ss.at[s], h_rs.at[s], edge_peer(s)) for s in range(6)]
    for c in grad_copies:
        c.start()
    igo[...] = input_grad(1)
    sum_z(0)
    sum_z(1)
    gather2(0)
    gather2(1)

    for c in grad_copies:
        c.wait()
    edges = egr[0].astype(F32)
    for s in range(1, 6):
        edges += egr[s].astype(F32)
    acc = igo[...] + gr[0].astype(F32) + gr[1].astype(F32)
    edge_hi = edges.astype(BF)
    edge_lo = (edges - edge_hi.astype(F32)).astype(BF)
    acc += dot(edge_hi, sel, TN) + dot(edge_lo, sel, TN)
    ig[...] = lanes_to_rows(acc)

    for h in range(2):
        for i in (1, 3, 2):
            gather3(h, i)
    for h in range(2):
        for i in (0, 1, 3, 2):
            gather_core(h, i)
    for h in range(2):
        for i in range(4):
            gc_copy(h, i, core, (me1[h] + 4 - i) % 4).wait_send()
        for i in (1, 2, 3):
            g3_copy(h, i, me1[h]).wait_send()


def write_back(out_v, ig_v, wg_v, out, ig, wg, sem):
    copies = [
        pltpu.make_async_copy(wg_v.at[n : n + 64], wg.at[n : n + 64], sem.at[n // 64])
        for n in range(0, C, 64)
    ]
    copies.append(pltpu.make_async_copy(out_v, out, sem.at[4]))
    copies.append(pltpu.make_async_copy(ig_v, ig, sem.at[5]))
    for c in copies:
        c.start()
    for c in copies:
        c.wait()


def per_device(features, weight, filter_table, row_range, basis_id, cotangent):
    vmem = pl.BlockSpec(memory_space=pltpu.VMEM)
    hbm = pl.BlockSpec(memory_space=pltpu.HBM)
    dma = pltpu.SemaphoreType.DMA
    scratch = [
        pltpu.VMEM((2, C, 2, LANES), BF),
        pltpu.VMEM((C, 256), BF),
        pltpu.VMEM((C, 256), BF),
        pltpu.SMEM((K, 5, 16), F32),
        pltpu.SMEM((2, N_ROWS), jnp.int32),
        pltpu.SMEM((5, N_ROWS), jnp.int32),
        pltpu.VMEM((C, C * K), BF),
        pltpu.VMEM((2, C, 256), BF),
        pltpu.VMEM((16, C), BF),
        pltpu.VMEM((6, 16, C), BF),
        pltpu.VMEM((K, 3, 256, 256), BF),
        pltpu.VMEM((K, 96, 256), BF),
        pltpu.VMEM((2, C * K, LANES), F32),
        pltpu.VMEM((C * K, 256), BF),
        pltpu.VMEM((K, C, 256), BF),
        pltpu.VMEM((2, C, 256), BF),
        pltpu.VMEM((2, C, 256), BF),
        pltpu.VMEM((6, 16, C), BF),
        pltpu.VMEM((6, 16, C), BF),
        pltpu.VMEM((2, 128, HALF), BF),
        pltpu.VMEM((2, 128, HALF), BF),
        pltpu.VMEM((2, 128, HALF), F32),
        pltpu.VMEM((2, 128, HALF), BF),
        pltpu.VMEM((2, 4, 32, HALF), BF),
        pltpu.VMEM((2, 4, 80, LANES), F32),
        pltpu.VMEM((2, 4, 80, LANES), BF),
        pltpu.VMEM((2, 4, 80, LANES), BF),
        pltpu.VMEM((2, NZ, 80, LANES), BF),
        pltpu.VMEM((2, 4, 80, LANES), BF),
        pltpu.VMEM((C, C * K), BF),
        pltpu.VMEM((C, 256), F32),
        dma((6,)),
        dma((2, 2)), dma((2, 2)), dma((6,)), dma((6,)), dma((2,)), dma((2,)), dma((6,)), dma((6,)),
        dma((2,)), dma((2,)),
        dma((2, 4)), dma((2, 4)), dma((2, 4)), dma((2, 4)), dma((2, NZ)), dma((2, NZ)),
        dma((2, 4)), dma((2, 4)), dma((2, 4)), dma((2, 4)), dma((2, 4)), dma((2, 4)),
    ]
    out, ig, wg = pl.pallas_call(
        kernel,
        out_shape=(
            pltpu.VMEM((C, 2, LANES), BF),
            pltpu.VMEM((C, 2, LANES), BF),
            pltpu.VMEM((C, C * K), F32),
        ),
        in_specs=[hbm] * 6,
        out_specs=(vmem, vmem, vmem),
        scratch_shapes=scratch,
        compiler_params=pltpu.CompilerParams(
            collective_id=0, has_side_effects=True, vmem_limit_bytes=56 * 1024 * 1024
        ),
    )(
        features,
        cotangent,
        weight,
        filter_table.transpose(1, 2, 0),
        row_range.T,
        basis_id.T,
    )
    return pl.pallas_call(
        write_back,
        out_shape=(
            jax.ShapeDtypeStruct((C, 2, LANES), BF),
            jax.ShapeDtypeStruct((C, 2, LANES), BF),
            jax.ShapeDtypeStruct((C, C * K), F32),
        ),
        in_specs=[vmem] * 3,
        out_specs=(hbm, hbm, hbm),
        scratch_shapes=[dma((6,))],
    )(*[pltpu.with_memory_space_constraint(v, pltpu.VMEM) for v in (out, ig, wg)])


def solution(mesh):
    in_specs = (P(None, "lat", "lon"), P(), P(), P(), P(), P(None, "lat", "lon"))
    out_specs = (P(None, "lat", "lon"), P(None, "lat", "lon"), P())
    return jax.shard_map(
        per_device, mesh=mesh, in_specs=in_specs, out_specs=out_specs, check_vma=False
    )
```

```python
import functools
import math

import jax
import jax.numpy as jnp
from jax import lax
from jax.experimental import pallas as pl
from jax.experimental.pallas import tpu as pltpu
from jax.sharding import PartitionSpec as P

BF = jnp.bfloat16
F32 = jnp.float32
MESH = pl.DeviceIdType.MESH
C = 256
K = 9
LANES = 128
NZ = 8
N_LAT, N_LON = 64, 4
N_ROWS = 128
CHANNELS = [(0, 144), (144, 256)]
COLUMNS = [(0, 1280), (1280, 2304)]
PIECE = [slice(0, 80), slice(80, 144)]
NEAR_FIRST = [1, 3, 4, 12, 5, 7, 13, 15, 2, 8, 6, 14, 9, 11, 10]
Z_FAR_FIRST = [4, 3, 5, 2, 6, 1, 7]
NT = (((1,), (1,)), ((), ()))
TN = (((0,), (0,)), ((), ()))
NN = (((1,), (0,)), ((), ()))


def dot(a, b, dims=NN):
    return lax.dot_general(a, b, dims, preferred_element_type=F32)


def kernel(
    feat_hbm, cot_hbm, w_hbm, table_hbm, rng_hbm, ids_hbm,
    out, ig, wg,
    raw, feat, cot, table, rng, ids, w, fx, e_send, e_recv, e_rows, bmat, bhal, big, bo, bgk, igp, gr, egs, egr,
    cs, cr, own, xs, xr, zr, ga, igo,
    in_sem, f_ss, f_rs, e_ss, e_rs, g_ss, g_rs, h_ss, h_rs, c_ss, c_rs,
    x_ss, x_rs, z_ss, z_rs, gx_ss, gx_rs, gc_ss, gc_rs,
):
    la, lo = lax.axis_index("lat"), lax.axis_index("lon")
    y, z, xh = la // 16, (la // 2) % 8, la % 2
    xl, core = lo // 2, lo % 2
    x = xh * 2 + xl
    sibling = (la, lo + 1 - 2 * core)
    me_n = y * 4 + x

    def lat_peer(dl):
        return (lax.rem(la + dl + N_LAT, N_LAT), lo)

    def edge_peer(s):
        dl, dc = s // 2 - 1, 2 * (s % 2) - 1
        return (lax.rem(la + dl + N_LAT, N_LAT), lax.rem(lo + dc + N_LON, N_LON))

    def plane(i, sign=1):
        return (y + 4 + sign * (i // 4)) % 4, (x + 4 + sign * (i % 4)) % 4

    def xy_peer(i):
        py, px = plane(i)
        return ((py * 8 + z) * 2 + px // 2, (px % 2) * 2 + core)

    def xy_index(i):
        py, px = plane(i)
        return py * 4 + px

    def from_index(i):
        py, px = plane(i, -1)
        return py * 4 + px

    def z_peer(i):
        return ((y * 8 + (z + i) % 8) * 2 + xh, lo)

    in_copies = [
        pltpu.make_async_copy(src, dst, in_sem.at[i])
        for i, (src, dst) in enumerate(
            [
                (feat_hbm, raw.at[0]),
                (table_hbm, table),
                (rng_hbm, rng),
                (ids_hbm, ids),
                (cot_hbm, raw.at[1]),
                (w_hbm, w),
            ]
        )
    ]
    for c in in_copies:
        c.start()

    barrier = pltpu.get_barrier_semaphore()
    peers = [lat_peer(-1), lat_peer(1)] + [edge_peer(s) for s in range(6)]
    peers += [xy_peer(i) for i in NEAR_FIRST if i != 2]
    peers += [z_peer(i) for i in range(1, NZ)]
    for peer in peers:
        pl.semaphore_signal(barrier, inc=1, device_id=peer, device_id_type=MESH)

    def rows_to_lanes(ref, dst):
        v = ref[...].astype(F32)
        dst[:, :LANES] = v[:, 0, :].astype(BF)
        dst[:, LANES:] = v[:, 1, :].astype(BF)

    def lanes_to_rows(v):
        return jnp.stack([v[:, :LANES], v[:, LANES:]], axis=1).astype(BF)

    in_copies[0].wait()
    rows_to_lanes(raw.at[0], feat)

    rho = lax.broadcasted_iota(jnp.int32, (16, 2 * LANES), 0)
    col = lax.broadcasted_iota(jnp.int32, (16, 2 * LANES), 1)
    edge_i = rho % 4
    edge_col = jnp.where(edge_i < 2, edge_i, edge_i + LANES - 4)
    sel = ((rho < 8) & (col == (rho // 4) * LANES + edge_col)).astype(F32).astype(BF)
    e_send[...] = dot(sel, feat[...], NT).astype(BF)

    pl.semaphore_wait(barrier, len(peers))

    def remote(src, dst, ss, rs, peer):
        return pltpu.make_async_remote_copy(
            src_ref=src, dst_ref=dst, send_sem=ss, recv_sem=rs, device_id=peer, device_id_type=MESH
        )

    half_rows = [slice(*c) for c in CHANNELS]
    feat_copies = [
        [
            remote(
                feat.at[half_rows[h]], fx.at[1, half_rows[h]], f_ss.at[h, 0], f_rs.at[h, 1], lat_peer(-1)
            ),
            remote(
                feat.at[half_rows[h]], fx.at[0, half_rows[h]], f_ss.at[h, 1], f_rs.at[h, 0], lat_peer(1)
            ),
        ]
        for h in range(2)
    ]
    edge_copies = [
        remote(e_send, e_recv.at[5 - s], e_ss.at[s], e_rs.at[5 - s], edge_peer(s)) for s in range(6)
    ]
    for c in feat_copies[0] + edge_copies:
        c.start()

    for c in in_copies[1:4]:
        c.wait()
    diag = lax.broadcasted_iota(jnp.int32, (LANES, LANES), 0) - lax.broadcasted_iota(
        jnp.int32, (LANES, LANES), 1
    ) + 2
    hr = lax.broadcasted_iota(jnp.int32, (16, LANES), 0)
    hp = lax.broadcasted_iota(jnp.int32, (16, LANES), 1)
    row_ids, row_act = [], []
    for t in range(2):
        g = la * 2 + t
        r0, r1_ = rng[0, g], rng[1, g]
        row_ids.append([ids[j, g] for j in range(5)])
        row_act.append(
            [
                (j >= r0) & (j < r1_) & (g + j - 2 >= 0) & (g + j - 2 < N_ROWS)
                for j in range(5)
            ]
        )
    zero_block = jnp.zeros((LANES, LANES), BF)

    def build(k, _):
        coef = [
            [
                [jnp.where(row_act[t][j], table[k, l, row_ids[t][j]], 0.0) for l in range(5)]
                for j in range(5)
            ]
            for t in range(2)
        ]
        for t in range(2):
            lanes = slice(t * LANES, (t + 1) * LANES)
            for e in range(6):
                j = e - t
                rows = slice((e % 2) * LANES, (e % 2 + 1) * LANES)
                if j < 0 or j > 4:
                    bmat[k, e // 2, rows, lanes] = zero_block
                    continue
                v = jnp.zeros((LANES, LANES), F32)
                for l in range(5):
                    v = jnp.where(diag == l, coef[t][j][l], v)
                bmat[k, e // 2, rows, lanes] = v.astype(BF)
            for s in range(6):
                v = jnp.zeros((16, LANES), F32)
                for r in range(2):
                    j = (s // 2) * 2 + r - t
                    if j < 0 or j > 4:
                        continue
                    if s % 2 == 0:
                        outer = (hr == r * 4 + 2) & (hp == 0) | (hr == r * 4 + 3) & (hp == 1)
                        inner = (hr == r * 4 + 3) & (hp == 0)
                        v = jnp.where(outer, coef[t][j][0], jnp.where(inner, coef[t][j][1], v))
                    else:
                        outer = (hr == r * 4) & (hp == 126) | (hr == r * 4 + 1) & (hp == 127)
                        inner = (hr == r * 4) & (hp == 127)
                        v = jnp.where(outer, coef[t][j][4], jnp.where(inner, coef[t][j][3], v))
                bhal[k, s * 16 : s * 16 + 16, lanes] = v.astype(BF)
        return 0

    lax.fori_loop(0, 4, build, 0)
    for c in feat_copies[0]:
        c.wait_send()
    for c in feat_copies[1]:
        c.start()
    lax.fori_loop(4, K, build, 0)

    in_copies[4].wait()
    rows_to_lanes(raw.at[1], cot)

    theirs = pl.ds(pl.multiple_of(128 * (1 - core), 128), 128)
    mine = pl.ds(pl.multiple_of(128 * core, 128), 128)

    def core_copy(h):
        cols = slice(*COLUMNS[h])
        return remote(cs.at[:, cols], cr.at[:, cols], c_ss.at[h], c_rs.at[h], sibling)

    def basis(h):
        hc = half_rows[h]
        for k in range(K):
            acc = dot(feat[hc, :], bmat[k, 1]) + dot(fx[0, hc, :], bmat[k, 0])
            acc += dot(fx[1, hc, :], bmat[k, 2]) + dot(e_rows[hc, :], bhal[k])
            rows = pl.ds(hc.start * K + k, hc.stop - hc.start, stride=K)
            big[0, rows, :] = acc[:, :LANES]
            big[1, rows, :] = acc[:, LANES:]
        for a in range(*COLUMNS[h], 256):
            rows = slice(a, a + 256)
            bo[rows, :LANES] = big[0, rows, :].astype(BF)
            bo[rows, LANES:] = big[1, rows, :].astype(BF)
            cs[:, rows] = dot(cot[theirs, :], bo[rows, :], NT).astype(BF)
        core_copy(h).start()

    def weight_rows(h):
        for a in range(*COLUMNS[h], 256):
            own[:, a : a + 256] = dot(cot[mine, :], bo[a : a + 256, :], NT)

    def xy_copy(h, i):
        src, dst = xs.at[xy_index(i), PIECE[h]], xr.at[i, PIECE[h]]
        return remote(src, dst, x_ss.at[h, i], x_rs.at[h, i], xy_peer(i))

    def z_copy(h, i, n):
        ref = zr.at[n, PIECE[h]]
        return remote(ref, ref, z_ss.at[h, i], z_rs.at[h, i], z_peer(i))

    def gx_copy(h, i, n):
        ref = ga.at[core, n, PIECE[h]]
        return remote(ref, ref, gx_ss.at[h, i], gx_rs.at[h, i], xy_peer(i))

    def gc_copy(h, i, c):
        ref = ga.at[c, from_index(i), PIECE[h]]
        return remote(ref, ref, gc_ss.at[h, i], gc_rs.at[h, i], sibling)

    def sent(copy, order, *args):
        for i in order:
            copy(0, i, *args).wait_send()

    def core_sum(h):
        core_copy(h).wait()
        cols = slice(*COLUMNS[h])
        v = own[:, cols] + cr[:, cols].astype(F32)
        tiles = [v[:, a : a + LANES].reshape(16, 8, LANES) for a in range(0, v.shape[1], LANES)]
        for m in range(0, len(tiles), 2):
            rows = slice(PIECE[h].start + 8 * m, PIECE[h].start + 8 * m + 16)
            xs[:, rows, :] = jnp.concatenate(tiles[m : m + 2], axis=1).astype(BF)
        if h == 1:
            sent(xy_copy, NEAR_FIRST)
        for i in reversed(NEAR_FIRST):
            xy_copy(h, i).start()

    def sum_xy(h):
        total = xs[me_n, PIECE[h], :].astype(F32)
        for i in NEAR_FIRST:
            xy_copy(h, i).wait_recv()
            total += xr[i, PIECE[h], :].astype(F32)
        zr[z, PIECE[h], :] = total.astype(BF)
        if h == 1:
            sent(z_copy, Z_FAR_FIRST, z)
        for i in Z_FAR_FIRST:
            z_copy(h, i, z).start()

    def sum_z(h):
        for i in range(1, NZ):
            z_copy(h, i, (z + 8 - i) % 8).wait_recv()
        total = zr[0, PIECE[h], :].astype(F32)
        for i in range(1, NZ):
            total += zr[i, PIECE[h], :].astype(F32)
        total *= F32(1.0 / math.sqrt(N_ROWS * N_LON * LANES))
        ga[core, me_n, PIECE[h], :] = total.astype(BF)
        gc_copy(h, 0, core).start()
        if h == 1:
            sent(gx_copy, NEAR_FIRST, me_n)
        for i in reversed(NEAR_FIRST):
            gx_copy(h, i, me_n).start()
        widen(h, core, me_n)

    def widen(h, c, n):
        v = ga[c, n, PIECE[h], :].astype(F32)
        rows = pl.ds(pl.multiple_of(128 * c + 8 * n, 8), 8)
        for m in range(v.shape[0] // 8):
            a = COLUMNS[h][0] + m * LANES
            wg[rows, a : a + LANES] = v[8 * m : 8 * m + 8]

    def gather_xy(h):
        for i in NEAR_FIRST:
            n = from_index(i)
            gx_copy(h, i, n).wait_recv()
            gc_copy(h, i, core).start()
            widen(h, core, n)

    def gather_core(h):
        for i in [0] + NEAR_FIRST:
            gc_copy(h, i, 1 - core).wait_recv()
            widen(h, 1 - core, from_index(i))

    for c in feat_copies[0]:
        c.wait_recv()
    for c in edge_copies:
        c.wait()
    e_rows[...] = jnp.transpose(e_recv[...].reshape(96, C).astype(F32)).astype(BF)
    basis(0)
    weight_rows(0)
    core_sum(0)
    for c in feat_copies[1]:
        c.wait()
    basis(1)
    weight_rows(1)
    core_sum(1)

    in_copies[5].wait()

    def basis_grad(m, _):
        cols = pl.ds(pl.multiple_of(m * 256, 256), 256)
        g = dot(w[:, cols], cot[...], TN)
        big[0, cols, :] = g[:, :LANES]
        big[1, cols, :] = g[:, LANES:]
        return 0

    lax.fori_loop(0, K, basis_grad, 0)
    for k in range(K):
        for t in range(2):
            bgk[k, :, t * LANES : (t + 1) * LANES] = big[t, pl.ds(k, C, stride=K), :].astype(BF)

    def input_grad(dl):
        acc = dot(bgk[0], bmat[0, dl], NT)
        for k in range(1, K):
            acc += dot(bgk[k], bmat[k, dl], NT)
        return acc

    igp[0] = input_grad(0).astype(BF)
    sum_xy(0)
    igp[1] = input_grad(2).astype(BF)
    acc = dot(bhal[0], bgk[0], NT)
    for k in range(1, K):
        acc += dot(bhal[k], bgk[k], NT)
    for s in range(6):
        egs[s] = acc[s * 16 : s * 16 + 16].astype(BF)
    grad_copies = [
        remote(igp.at[0], gr.at[1], g_ss.at[0], g_rs.at[1], lat_peer(-1)),
        remote(igp.at[1], gr.at[0], g_ss.at[1], g_rs.at[0], lat_peer(1)),
    ] + [remote(egs.at[s], egr.at[s], h_ss.at[s], h_rs.at[s], edge_peer(s)) for s in range(6)]
    for c in grad_copies:
        c.start()
    igo[...] = input_grad(1)
    sum_xy(1)

    acc = dot(w[:, :256], bo[:256, :])
    for m in range(1, K):
        acc += dot(w[:, m * 256 : m * 256 + 256], bo[m * 256 : m * 256 + 256, :])
    out[...] = lanes_to_rows(acc)
    sum_z(0)
    sum_z(1)
    gather_xy(0)

    for c in grad_copies:
        c.wait()
    edges = egr[0].astype(F32)
    for s in range(1, 6):
        edges += egr[s].astype(F32)
    acc = igo[...] + gr[0].astype(F32) + gr[1].astype(F32)
    edge_hi = edges.astype(BF)
    edge_lo = (edges - edge_hi.astype(F32)).astype(BF)
    acc += dot(edge_hi, sel, TN) + dot(edge_lo, sel, TN)
    ig[...] = lanes_to_rows(acc)

    gather_core(0)
    gather_xy(1)
    gather_core(1)
    for i in NEAR_FIRST:
        xy_copy(1, i).wait_send()
        gx_copy(1, i, me_n).wait_send()
    for i in Z_FAR_FIRST:
        z_copy(1, i, z).wait_send()
    for h in range(2):
        for i in [0] + NEAR_FIRST:
            gc_copy(h, i, core).wait_send()


def write_back(out_v, ig_v, wg_v, out, ig, wg, sem):
    copies = [
        pltpu.make_async_copy(wg_v.at[n : n + 64], wg.at[n : n + 64], sem.at[n // 64])
        for n in range(0, C, 64)
    ]
    copies.append(pltpu.make_async_copy(out_v, out, sem.at[4]))
    copies.append(pltpu.make_async_copy(ig_v, ig, sem.at[5]))
    for c in copies:
        c.start()
    for c in copies:
        c.wait()


def per_device(features, weight, filter_table, row_range, basis_id, cotangent):
    vmem = pl.BlockSpec(memory_space=pltpu.VMEM)
    hbm = pl.BlockSpec(memory_space=pltpu.HBM)
    dma = pltpu.SemaphoreType.DMA
    scratch = [
        pltpu.VMEM((2, C, 2, LANES), BF),
        pltpu.VMEM((C, 256), BF),
        pltpu.VMEM((C, 256), BF),
        pltpu.SMEM((K, 5, 16), F32),
        pltpu.SMEM((2, N_ROWS), jnp.int32),
        pltpu.SMEM((5, N_ROWS), jnp.int32),
        pltpu.VMEM((C, C * K), BF),
        pltpu.VMEM((2, C, 256), BF),
        pltpu.VMEM((16, C), BF),
        pltpu.VMEM((6, 16, C), BF),
        pltpu.VMEM((C, 96), BF),
        pltpu.VMEM((K, 3, 256, 256), BF),
        pltpu.VMEM((K, 96, 256), BF),
        pltpu.VMEM((2, C * K, LANES), F32),
        pltpu.VMEM((C * K, 256), BF),
        pltpu.VMEM((K, C, 256), BF),
        pltpu.VMEM((2, C, 256), BF),
        pltpu.VMEM((2, C, 256), BF),
        pltpu.VMEM((6, 16, C), BF),
        pltpu.VMEM((6, 16, C), BF),
        pltpu.VMEM((128, C * K), BF),
        pltpu.VMEM((128, C * K), BF),
        pltpu.VMEM((128, C * K), F32),
        pltpu.VMEM((16, 144, LANES), BF),
        pltpu.VMEM((16, 144, LANES), BF),
        pltpu.VMEM((NZ, 144, LANES), BF),
        pltpu.VMEM((2, 16, 144, LANES), BF),
        pltpu.VMEM((C, 256), F32),
        dma((6,)),
        dma((2, 2)), dma((2, 2)), dma((6,)), dma((6,)), dma((2,)), dma((2,)), dma((6,)), dma((6,)),
        dma((2,)), dma((2,)),
        dma((2, 16)), dma((2, 16)), dma((2, NZ)), dma((2, NZ)),
        dma((2, 16)), dma((2, 16)), dma((2, 16)), dma((2, 16)),
    ]
    out, ig, wg = pl.pallas_call(
        kernel,
        out_shape=(
            pltpu.VMEM((C, 2, LANES), BF),
            pltpu.VMEM((C, 2, LANES), BF),
            pltpu.VMEM((C, C * K), F32),
        ),
        in_specs=[hbm] * 6,
        out_specs=(vmem, vmem, vmem),
        scratch_shapes=scratch,
        compiler_params=pltpu.CompilerParams(
            collective_id=0, has_side_effects=True, vmem_limit_bytes=56 * 1024 * 1024
        ),
    )(
        features,
        cotangent,
        weight,
        filter_table.transpose(1, 2, 0),
        row_range.T,
        basis_id.T,
    )
    return pl.pallas_call(
        write_back,
        out_shape=(
            jax.ShapeDtypeStruct((C, 2, LANES), BF),
            jax.ShapeDtypeStruct((C, 2, LANES), BF),
            jax.ShapeDtypeStruct((C, C * K), F32),
        ),
        in_specs=[vmem] * 3,
        out_specs=(hbm, hbm, hbm),
        scratch_shapes=[dma((6,))],
    )(*[pltpu.with_memory_space_constraint(v, pltpu.VMEM) for v in (out, ig, wg)])


def solution(mesh):
    in_specs = (P(None, "lat", "lon"), P(), P(), P(), P(), P(None, "lat", "lon"))
    out_specs = (P(None, "lat", "lon"), P(None, "lat", "lon"), P())
    return jax.shard_map(
        per_device, mesh=mesh, in_specs=in_specs, out_specs=out_specs, check_vma=False
    )
```

```python
import functools
import math

import jax
import jax.numpy as jnp
from jax import lax
from jax.experimental import pallas as pl
from jax.experimental.pallas import tpu as pltpu
from jax.sharding import PartitionSpec as P

BF = jnp.bfloat16
F32 = jnp.float32
MESH = pl.DeviceIdType.MESH
C = 256
K = 9
LANES = 128
NZ = 8
N_LAT, N_LON = 64, 4
N_ROWS = 128
CHANNELS = [(0, 144), (144, 256)]
COLUMNS = [(0, 1280), (1280, 2304)]
PIECE = [slice(0, 80), slice(80, 144)]
NEAR_FIRST = [1, 3, 4, 12, 5, 7, 13, 15, 2, 8, 6, 14, 9, 11, 10]
Z_FAR_FIRST = [4, 3, 5, 2, 6, 1, 7]
NT = (((1,), (1,)), ((), ()))
TN = (((0,), (0,)), ((), ()))
NN = (((1,), (0,)), ((), ()))


def dot(a, b, dims=NN):
    return lax.dot_general(a, b, dims, preferred_element_type=F32)


def kernel(
    feat_hbm, cot_hbm, w_hbm, table_hbm, rng_hbm, ids_hbm,
    out, ig, wg,
    raw, feat, cot, table, rng, ids, w, fx, e_send, e_recv, e_rows, bmat, bhal, big, bo, bgk, igp, gr, egs, egr,
    cs, cr, own, xs, xr, zr, ga, igo,
    in_sem, f_ss, f_rs, e_ss, e_rs, g_ss, g_rs, h_ss, h_rs, c_ss, c_rs,
    x_ss, x_rs, z_ss, z_rs, gx_ss, gx_rs, gc_ss, gc_rs,
):
    la, lo = lax.axis_index("lat"), lax.axis_index("lon")
    y, z, xh = la // 16, (la // 2) % 8, la % 2
    xl, core = lo // 2, lo % 2
    x = xh * 2 + xl
    sibling = (la, lo + 1 - 2 * core)
    me_n = y * 4 + x

    def lat_peer(dl):
        return (lax.rem(la + dl + N_LAT, N_LAT), lo)

    def edge_peer(s):
        dl, dc = s // 2 - 1, 2 * (s % 2) - 1
        return (lax.rem(la + dl + N_LAT, N_LAT), lax.rem(lo + dc + N_LON, N_LON))

    def plane(i, sign=1):
        return (y + 4 + sign * (i // 4)) % 4, (x + 4 + sign * (i % 4)) % 4

    def xy_peer(i):
        py, px = plane(i)
        return ((py * 8 + z) * 2 + px // 2, (px % 2) * 2 + core)

    def xy_index(i):
        py, px = plane(i)
        return py * 4 + px

    def from_index(i):
        py, px = plane(i, -1)
        return py * 4 + px

    def z_peer(i):
        return ((y * 8 + (z + i) % 8) * 2 + xh, lo)

    in_copies = [
        pltpu.make_async_copy(src, dst, in_sem.at[i])
        for i, (src, dst) in enumerate(
            [
                (feat_hbm, raw.at[0]),
                (table_hbm, table),
                (rng_hbm, rng),
                (ids_hbm, ids),
                (cot_hbm, raw.at[1]),
                (w_hbm, w),
            ]
        )
    ]
    for c in in_copies:
        c.start()

    barrier = pltpu.get_barrier_semaphore()
    peers = [lat_peer(-1), lat_peer(1)] + [edge_peer(s) for s in range(6)]
    peers += [xy_peer(i) for i in NEAR_FIRST if i != 2]
    peers += [z_peer(i) for i in range(1, NZ)]
    for peer in peers:
        pl.semaphore_signal(barrier, inc=1, device_id=peer, device_id_type=MESH)

    def rows_to_lanes(ref, dst):
        v = ref[...].astype(F32)
        dst[:, :LANES] = v[:, 0, :].astype(BF)
        dst[:, LANES:] = v[:, 1, :].astype(BF)

    def lanes_to_rows(v):
        return jnp.stack([v[:, :LANES], v[:, LANES:]], axis=1).astype(BF)

    in_copies[0].wait()
    rows_to_lanes(raw.at[0], feat)

    rho = lax.broadcasted_iota(jnp.int32, (16, 2 * LANES), 0)
    col = lax.broadcasted_iota(jnp.int32, (16, 2 * LANES), 1)
    edge_i = rho % 4
    edge_col = jnp.where(edge_i < 2, edge_i, edge_i + LANES - 4)
    sel = ((rho < 8) & (col == (rho // 4) * LANES + edge_col)).astype(F32).astype(BF)
    e_send[...] = dot(sel, feat[...], NT).astype(BF)

    pl.semaphore_wait(barrier, len(peers))

    def remote(src, dst, ss, rs, peer):
        return pltpu.make_async_remote_copy(
            src_ref=src, dst_ref=dst, send_sem=ss, recv_sem=rs, device_id=peer, device_id_type=MESH
        )

    half_rows = [slice(*c) for c in CHANNELS]
    feat_copies = [
        [
            remote(
                feat.at[half_rows[h]], fx.at[1, half_rows[h]], f_ss.at[h, 0], f_rs.at[h, 1], lat_peer(-1)
            ),
            remote(
                feat.at[half_rows[h]], fx.at[0, half_rows[h]], f_ss.at[h, 1], f_rs.at[h, 0], lat_peer(1)
            ),
        ]
        for h in range(2)
    ]
    edge_copies = [
        remote(e_send, e_recv.at[5 - s], e_ss.at[s], e_rs.at[5 - s], edge_peer(s)) for s in range(6)
    ]
    for c in feat_copies[0] + edge_copies:
        c.start()

    for c in in_copies[1:4]:
        c.wait()
    diag = lax.broadcasted_iota(jnp.int32, (LANES, LANES), 0) - lax.broadcasted_iota(
        jnp.int32, (LANES, LANES), 1
    ) + 2
    hr = lax.broadcasted_iota(jnp.int32, (16, LANES), 0)
    hp = lax.broadcasted_iota(jnp.int32, (16, LANES), 1)
    row_ids, row_act = [], []
    for t in range(2):
        g = la * 2 + t
        r0, r1_ = rng[0, g], rng[1, g]
        row_ids.append([ids[j, g] for j in range(5)])
        row_act.append(
            [
                (j >= r0) & (j < r1_) & (g + j - 2 >= 0) & (g + j - 2 < N_ROWS)
                for j in range(5)
            ]
        )
    zero_block = jnp.zeros((LANES, LANES), BF)

    def build(k, _):
        coef = [
            [
                [jnp.where(row_act[t][j], table[k, l, row_ids[t][j]], 0.0) for l in range(5)]
                for j in range(5)
            ]
            for t in range(2)
        ]
        for t in range(2):
            lanes = slice(t * LANES, (t + 1) * LANES)
            for e in range(6):
                j = e - t
                rows = slice((e % 2) * LANES, (e % 2 + 1) * LANES)
                if j < 0 or j > 4:
                    bmat[k, e // 2, rows, lanes] = zero_block
                    continue
                v = jnp.zeros((LANES, LANES), F32)
                for l in range(5):
                    v = jnp.where(diag == l, coef[t][j][l], v)
                bmat[k, e // 2, rows, lanes] = v.astype(BF)
            for s in range(6):
                v = jnp.zeros((16, LANES), F32)
                for r in range(2):
                    j = (s // 2) * 2 + r - t
                    if j < 0 or j > 4:
                        continue
                    if s % 2 == 0:
                        outer = (hr == r * 4 + 2) & (hp == 0) | (hr == r * 4 + 3) & (hp == 1)
                        inner = (hr == r * 4 + 3) & (hp == 0)
                        v = jnp.where(outer, coef[t][j][0], jnp.where(inner, coef[t][j][1], v))
                    else:
                        outer = (hr == r * 4) & (hp == 126) | (hr == r * 4 + 1) & (hp == 127)
                        inner = (hr == r * 4) & (hp == 127)
                        v = jnp.where(outer, coef[t][j][4], jnp.where(inner, coef[t][j][3], v))
                bhal[k, s * 16 : s * 16 + 16, lanes] = v.astype(BF)
        return 0

    lax.fori_loop(0, 4, build, 0)
    for c in feat_copies[0]:
        c.wait_send()
    for c in feat_copies[1]:
        c.start()
    lax.fori_loop(4, K, build, 0)

    in_copies[4].wait()
    rows_to_lanes(raw.at[1], cot)

    theirs = pl.ds(pl.multiple_of(128 * (1 - core), 128), 128)
    mine = pl.ds(pl.multiple_of(128 * core, 128), 128)

    def core_copy(h):
        cols = slice(*COLUMNS[h])
        return remote(cs.at[:, cols], cr.at[:, cols], c_ss.at[h], c_rs.at[h], sibling)

    def basis(h):
        hc = half_rows[h]
        for k in range(K):
            acc = dot(feat[hc, :], bmat[k, 1]) + dot(fx[0, hc, :], bmat[k, 0])
            acc += dot(fx[1, hc, :], bmat[k, 2]) + dot(e_rows[hc, :], bhal[k])
            rows = pl.ds(hc.start * K + k, hc.stop - hc.start, stride=K)
            big[0, rows, :] = acc[:, :LANES]
            big[1, rows, :] = acc[:, LANES:]
        for a in range(*COLUMNS[h], 256):
            rows = slice(a, a + 256)
            bo[rows, :LANES] = big[0, rows, :].astype(BF)
            bo[rows, LANES:] = big[1, rows, :].astype(BF)
            cs[:, rows] = dot(cot[theirs, :], bo[rows, :], NT).astype(BF)
        core_copy(h).start()

    def weight_rows(h):
        for a in range(*COLUMNS[h], 256):
            own[:, a : a + 256] = dot(cot[mine, :], bo[a : a + 256, :], NT)

    def xy_copy(h, i):
        src, dst = xs.at[xy_index(i), PIECE[h]], xr.at[i, PIECE[h]]
        return remote(src, dst, x_ss.at[h, i], x_rs.at[h, i], xy_peer(i))

    def z_copy(h, i, n):
        ref = zr.at[n, PIECE[h]]
        return remote(ref, ref, z_ss.at[h, i], z_rs.at[h, i], z_peer(i))

    def gx_copy(h, i, n):
        ref = ga.at[core, n, PIECE[h]]
        return remote(ref, ref, gx_ss.at[h, i], gx_rs.at[h, i], xy_peer(i))

    def gc_copy(h, i, c):
        ref = ga.at[c, from_index(i), PIECE[h]]
        return remote(ref, ref, gc_ss.at[h, i], gc_rs.at[h, i], sibling)

    def sent(copy, order, *args):
        for i in order:
            copy(0, i, *args).wait_send()

    def core_sum(h):
        core_copy(h).wait()
        cols = slice(*COLUMNS[h])
        v = own[:, cols] + cr[:, cols].astype(F32)
        tiles = [v[:, a : a + LANES].reshape(16, 8, LANES) for a in range(0, v.shape[1], LANES)]
        for m in range(0, len(tiles), 2):
            rows = slice(PIECE[h].start + 8 * m, PIECE[h].start + 8 * m + 16)
            xs[:, rows, :] = jnp.concatenate(tiles[m : m + 2], axis=1).astype(BF)
        for i in reversed(NEAR_FIRST):
            xy_copy(h, i).start()

    def sum_xy(h):
        total = xs[me_n, PIECE[h], :].astype(F32)
        for i in NEAR_FIRST:
            xy_copy(h, i).wait_recv()
            total += xr[i, PIECE[h], :].astype(F32)
        zr[z, PIECE[h], :] = total.astype(BF)
        if h == 1:
            sent(z_copy, Z_FAR_FIRST, z)
        for i in Z_FAR_FIRST:
            z_copy(h, i, z).start()

    def sum_z(h):
        for i in range(1, NZ):
            z_copy(h, i, (z + 8 - i) % 8).wait_recv()
        total = zr[0, PIECE[h], :].astype(F32)
        for i in range(1, NZ):
            total += zr[i, PIECE[h], :].astype(F32)
        total *= F32(1.0 / math.sqrt(N_ROWS * N_LON * LANES))
        ga[core, me_n, PIECE[h], :] = total.astype(BF)
        gc_copy(h, 0, core).start()
        if h == 1:
            sent(gx_copy, NEAR_FIRST, me_n)
        for i in reversed(NEAR_FIRST):
            gx_copy(h, i, me_n).start()
        widen(h, core, me_n)

    def widen(h, c, n):
        v = ga[c, n, PIECE[h], :].astype(F32)
        rows = pl.ds(pl.multiple_of(128 * c + 8 * n, 8), 8)
        for m in range(v.shape[0] // 8):
            a = COLUMNS[h][0] + m * LANES
            wg[rows, a : a + LANES] = v[8 * m : 8 * m + 8]

    def gather_xy(h):
        for i in NEAR_FIRST:
            n = from_index(i)
            gx_copy(h, i, n).wait_recv()
            gc_copy(h, i, core).start()
            widen(h, core, n)

    def gather_core(h):
        for i in [0] + NEAR_FIRST:
            gc_copy(h, i, 1 - core).wait_recv()
            widen(h, 1 - core, from_index(i))

    for c in feat_copies[0]:
        c.wait_recv()
    for c in edge_copies:
        c.wait()
    e_rows[...] = jnp.transpose(e_recv[...].reshape(96, C).astype(F32)).astype(BF)
    basis(0)
    weight_rows(0)
    core_sum(0)
    for c in feat_copies[1]:
        c.wait()
    basis(1)
    weight_rows(1)
    core_sum(1)

    in_copies[5].wait()

    def basis_grad(m, _):
        cols = pl.ds(pl.multiple_of(m * 256, 256), 256)
        g = dot(w[:, cols], cot[...], TN)
        big[0, cols, :] = g[:, :LANES]
        big[1, cols, :] = g[:, LANES:]
        return 0

    lax.fori_loop(0, K, basis_grad, 0)
    for k in range(K):
        for t in range(2):
            bgk[k, :, t * LANES : (t + 1) * LANES] = big[t, pl.ds(k, C, stride=K), :].astype(BF)

    def input_grad(dl):
        acc = dot(bgk[0], bmat[0, dl], NT)
        for k in range(1, K):
            acc += dot(bgk[k], bmat[k, dl], NT)
        return acc

    igp[0] = input_grad(0).astype(BF)
    sum_xy(0)
    igp[1] = input_grad(2).astype(BF)
    acc = dot(bhal[0], bgk[0], NT)
    for k in range(1, K):
        acc += dot(bhal[k], bgk[k], NT)
    for s in range(6):
        egs[s] = acc[s * 16 : s * 16 + 16].astype(BF)
    grad_copies = [
        remote(igp.at[0], gr.at[1], g_ss.at[0], g_rs.at[1], lat_peer(-1)),
        remote(igp.at[1], gr.at[0], g_ss.at[1], g_rs.at[0], lat_peer(1)),
    ] + [remote(egs.at[s], egr.at[s], h_ss.at[s], h_rs.at[s], edge_peer(s)) for s in range(6)]
    for c in grad_copies:
        c.start()
    igo[...] = input_grad(1)
    sum_xy(1)

    acc = dot(w[:, :256], bo[:256, :])
    for m in range(1, K):
        acc += dot(w[:, m * 256 : m * 256 + 256], bo[m * 256 : m * 256 + 256, :])
    out[...] = lanes_to_rows(acc)
    sum_z(0)
    sum_z(1)
    gather_xy(0)

    for c in grad_copies:
        c.wait()
    edges = egr[0].astype(F32)
    for s in range(1, 6):
        edges += egr[s].astype(F32)
    acc = igo[...] + gr[0].astype(F32) + gr[1].astype(F32)
    edge_hi = edges.astype(BF)
    edge_lo = (edges - edge_hi.astype(F32)).astype(BF)
    acc += dot(edge_hi, sel, TN) + dot(edge_lo, sel, TN)
    ig[...] = lanes_to_rows(acc)

    gather_core(0)
    gather_xy(1)
    gather_core(1)
    for i in NEAR_FIRST:
        xy_copy(0, i).wait_send()
        xy_copy(1, i).wait_send()
        gx_copy(1, i, me_n).wait_send()
    for i in Z_FAR_FIRST:
        z_copy(1, i, z).wait_send()
    for h in range(2):
        for i in [0] + NEAR_FIRST:
            gc_copy(h, i, core).wait_send()


def write_back(out_v, ig_v, wg_v, out, ig, wg, sem):
    copies = [
        pltpu.make_async_copy(wg_v.at[n : n + 64], wg.at[n : n + 64], sem.at[n // 64])
        for n in range(0, C, 64)
    ]
    copies.append(pltpu.make_async_copy(out_v, out, sem.at[4]))
    copies.append(pltpu.make_async_copy(ig_v, ig, sem.at[5]))
    for c in copies:
        c.start()
    for c in copies:
        c.wait()


def per_device(features, weight, filter_table, row_range, basis_id, cotangent):
    vmem = pl.BlockSpec(memory_space=pltpu.VMEM)
    hbm = pl.BlockSpec(memory_space=pltpu.HBM)
    dma = pltpu.SemaphoreType.DMA
    scratch = [
        pltpu.VMEM((2, C, 2, LANES), BF),
        pltpu.VMEM((C, 256), BF),
        pltpu.VMEM((C, 256), BF),
        pltpu.SMEM((K, 5, 16), F32),
        pltpu.SMEM((2, N_ROWS), jnp.int32),
        pltpu.SMEM((5, N_ROWS), jnp.int32),
        pltpu.VMEM((C, C * K), BF),
        pltpu.VMEM((2, C, 256), BF),
        pltpu.VMEM((16, C), BF),
        pltpu.VMEM((6, 16, C), BF),
        pltpu.VMEM((C, 96), BF),
        pltpu.VMEM((K, 3, 256, 256), BF),
        pltpu.VMEM((K, 96, 256), BF),
        pltpu.VMEM((2, C * K, LANES), F32),
        pltpu.VMEM((C * K, 256), BF),
        pltpu.VMEM((K, C, 256), BF),
        pltpu.VMEM((2, C, 256), BF),
        pltpu.VMEM((2, C, 256), BF),
        pltpu.VMEM((6, 16, C), BF),
        pltpu.VMEM((6, 16, C), BF),
        pltpu.VMEM((128, C * K), BF),
        pltpu.VMEM((128, C * K), BF),
        pltpu.VMEM((128, C * K), F32),
        pltpu.VMEM((16, 144, LANES), BF),
        pltpu.VMEM((16, 144, LANES), BF),
        pltpu.VMEM((NZ, 144, LANES), BF),
        pltpu.VMEM((2, 16, 144, LANES), BF),
        pltpu.VMEM((C, 256), F32),
        dma((6,)),
        dma((2, 2)), dma((2, 2)), dma((6,)), dma((6,)), dma((2,)), dma((2,)), dma((6,)), dma((6,)),
        dma((2,)), dma((2,)),
        dma((2, 16)), dma((2, 16)), dma((2, NZ)), dma((2, NZ)),
        dma((2, 16)), dma((2, 16)), dma((2, 16)), dma((2, 16)),
    ]
    out, ig, wg = pl.pallas_call(
        kernel,
        out_shape=(
            pltpu.VMEM((C, 2, LANES), BF),
            pltpu.VMEM((C, 2, LANES), BF),
            pltpu.VMEM((C, C * K), F32),
        ),
        in_specs=[hbm] * 6,
        out_specs=(vmem, vmem, vmem),
        scratch_shapes=scratch,
        compiler_params=pltpu.CompilerParams(
            collective_id=0, has_side_effects=True, vmem_limit_bytes=56 * 1024 * 1024
        ),
    )(
        features,
        cotangent,
        weight,
        filter_table.transpose(1, 2, 0),
        row_range.T,
        basis_id.T,
    )
    return pl.pallas_call(
        write_back,
        out_shape=(
            jax.ShapeDtypeStruct((C, 2, LANES), BF),
            jax.ShapeDtypeStruct((C, 2, LANES), BF),
            jax.ShapeDtypeStruct((C, C * K), F32),
        ),
        in_specs=[vmem] * 3,
        out_specs=(hbm, hbm, hbm),
        scratch_shapes=[dma((6,))],
    )(*[pltpu.with_memory_space_constraint(v, pltpu.VMEM) for v in (out, ig, wg)])


def solution(mesh):
    in_specs = (P(None, "lat", "lon"), P(), P(), P(), P(), P(None, "lat", "lon"))
    out_specs = (P(None, "lat", "lon"), P(None, "lat", "lon"), P())
    return jax.shard_map(
        per_device, mesh=mesh, in_specs=in_specs, out_specs=out_specs, check_vma=False
    )
```

```python
import functools
import math

import jax
import jax.numpy as jnp
from jax import lax
from jax.experimental import pallas as pl
from jax.experimental.pallas import tpu as pltpu
from jax.sharding import PartitionSpec as P

BF = jnp.bfloat16
F32 = jnp.float32
MESH = pl.DeviceIdType.MESH
C = 256
K = 9
LANES = 128
NZ = 8
N_LAT, N_LON = 64, 4
N_ROWS = 128
CHANNELS = [(0, 144), (144, 256)]
COLUMNS = [(0, 1280), (1280, 2304)]
PIECE = [slice(0, 80), slice(80, 144)]
NEAR_FIRST = [1, 3, 4, 12, 5, 7, 13, 15, 2, 8, 6, 14, 9, 11, 10]
Z_FAR_FIRST = [4, 3, 5, 2, 6, 1, 7]
NT = (((1,), (1,)), ((), ()))
TN = (((0,), (0,)), ((), ()))
NN = (((1,), (0,)), ((), ()))


def dot(a, b, dims=NN):
    return lax.dot_general(a, b, dims, preferred_element_type=F32)


def kernel(
    feat_hbm, cot_hbm, w_hbm, table_hbm, rng_hbm, ids_hbm,
    out, ig, wg,
    raw, feat, cot, table, rng, ids, w, fx, e_send, e_recv, e_rows, bmat, bhal, big, bo, bgk, igp, gr, egs, egr,
    cs, cr, own, xs, xr, zr, ga, igo,
    in_sem, f_ss, f_rs, e_ss, e_rs, g_ss, g_rs, h_ss, h_rs, c_ss, c_rs,
    x_ss, x_rs, z_ss, z_rs, gx_ss, gx_rs, gc_ss, gc_rs,
):
    la, lo = lax.axis_index("lat"), lax.axis_index("lon")
    y, z, xh = la // 16, (la // 2) % 8, la % 2
    xl, core = lo // 2, lo % 2
    x = xh * 2 + xl
    sibling = (la, lo + 1 - 2 * core)
    me_n = y * 4 + x

    def lat_peer(dl):
        return (lax.rem(la + dl + N_LAT, N_LAT), lo)

    def edge_peer(s):
        dl, dc = s // 2 - 1, 2 * (s % 2) - 1
        return (lax.rem(la + dl + N_LAT, N_LAT), lax.rem(lo + dc + N_LON, N_LON))

    def plane(i, sign=1):
        return (y + 4 + sign * (i // 4)) % 4, (x + 4 + sign * (i % 4)) % 4

    def xy_peer(i):
        py, px = plane(i)
        return ((py * 8 + z) * 2 + px // 2, (px % 2) * 2 + core)

    def xy_index(i):
        py, px = plane(i)
        return py * 4 + px

    def from_index(i):
        py, px = plane(i, -1)
        return py * 4 + px

    def z_peer(i):
        return ((y * 8 + (z + i) % 8) * 2 + xh, lo)

    in_copies = [
        pltpu.make_async_copy(src, dst, in_sem.at[i])
        for i, (src, dst) in enumerate(
            [
                (feat_hbm, raw.at[0]),
                (table_hbm, table),
                (rng_hbm, rng),
                (ids_hbm, ids),
                (cot_hbm, raw.at[1]),
                (w_hbm, w),
            ]
        )
    ]
    for c in in_copies:
        c.start()

    barrier = pltpu.get_barrier_semaphore()
    peers = [lat_peer(-1), lat_peer(1)] + [edge_peer(s) for s in range(6)]
    peers += [xy_peer(i) for i in NEAR_FIRST if i != 2]
    peers += [z_peer(i) for i in range(1, NZ)]
    for peer in peers:
        pl.semaphore_signal(barrier, inc=1, device_id=peer, device_id_type=MESH)

    def rows_to_lanes(ref, dst):
        v = ref[...].astype(F32)
        dst[:, :LANES] = v[:, 0, :].astype(BF)
        dst[:, LANES:] = v[:, 1, :].astype(BF)

    def lanes_to_rows(v):
        return jnp.stack([v[:, :LANES], v[:, LANES:]], axis=1).astype(BF)

    in_copies[0].wait()
    rows_to_lanes(raw.at[0], feat)

    rho = lax.broadcasted_iota(jnp.int32, (16, 2 * LANES), 0)
    col = lax.broadcasted_iota(jnp.int32, (16, 2 * LANES), 1)
    edge_i = rho % 4
    edge_col = jnp.where(edge_i < 2, edge_i, edge_i + LANES - 4)
    sel = ((rho < 8) & (col == (rho // 4) * LANES + edge_col)).astype(F32).astype(BF)
    e_send[...] = dot(sel, feat[...], NT).astype(BF)

    pl.semaphore_wait(barrier, len(peers))

    def remote(src, dst, ss, rs, peer):
        return pltpu.make_async_remote_copy(
            src_ref=src, dst_ref=dst, send_sem=ss, recv_sem=rs, device_id=peer, device_id_type=MESH
        )

    half_rows = [slice(*c) for c in CHANNELS]
    feat_copies = [
        [
            remote(
                feat.at[half_rows[h]], fx.at[1, half_rows[h]], f_ss.at[h, 0], f_rs.at[h, 1], lat_peer(-1)
            ),
            remote(
                feat.at[half_rows[h]], fx.at[0, half_rows[h]], f_ss.at[h, 1], f_rs.at[h, 0], lat_peer(1)
            ),
        ]
        for h in range(2)
    ]
    edge_copies = [
        remote(e_send, e_recv.at[5 - s], e_ss.at[s], e_rs.at[5 - s], edge_peer(s)) for s in range(6)
    ]
    for c in feat_copies[0] + edge_copies:
        c.start()

    for c in in_copies[1:4]:
        c.wait()
    diag = lax.broadcasted_iota(jnp.int32, (LANES, LANES), 0) - lax.broadcasted_iota(
        jnp.int32, (LANES, LANES), 1
    ) + 2
    hr = lax.broadcasted_iota(jnp.int32, (16, LANES), 0)
    hp = lax.broadcasted_iota(jnp.int32, (16, LANES), 1)
    row_ids, row_act = [], []
    for t in range(2):
        g = la * 2 + t
        r0, r1_ = rng[0, g], rng[1, g]
        row_ids.append([ids[j, g] for j in range(5)])
        row_act.append(
            [
                (j >= r0) & (j < r1_) & (g + j - 2 >= 0) & (g + j - 2 < N_ROWS)
                for j in range(5)
            ]
        )
    zero_block = jnp.zeros((LANES, LANES), BF)

    def build(k, _):
        coef = [
            [
                [jnp.where(row_act[t][j], table[k, l, row_ids[t][j]], 0.0) for l in range(5)]
                for j in range(5)
            ]
            for t in range(2)
        ]
        for t in range(2):
            lanes = slice(t * LANES, (t + 1) * LANES)
            for e in range(6):
                j = e - t
                rows = slice((e % 2) * LANES, (e % 2 + 1) * LANES)
                if j < 0 or j > 4:
                    bmat[k, e // 2, rows, lanes] = zero_block
                    continue
                v = jnp.zeros((LANES, LANES), F32)
                for l in range(5):
                    v = jnp.where(diag == l, coef[t][j][l], v)
                bmat[k, e // 2, rows, lanes] = v.astype(BF)
            for s in range(6):
                v = jnp.zeros((16, LANES), F32)
                for r in range(2):
                    j = (s // 2) * 2 + r - t
                    if j < 0 or j > 4:
                        continue
                    if s % 2 == 0:
                        outer = (hr == r * 4 + 2) & (hp == 0) | (hr == r * 4 + 3) & (hp == 1)
                        inner = (hr == r * 4 + 3) & (hp == 0)
                        v = jnp.where(outer, coef[t][j][0], jnp.where(inner, coef[t][j][1], v))
                    else:
                        outer = (hr == r * 4) & (hp == 126) | (hr == r * 4 + 1) & (hp == 127)
                        inner = (hr == r * 4) & (hp == 127)
                        v = jnp.where(outer, coef[t][j][4], jnp.where(inner, coef[t][j][3], v))
                bhal[k, s * 16 : s * 16 + 16, lanes] = v.astype(BF)
        return 0

    lax.fori_loop(0, 4, build, 0)
    for c in feat_copies[0]:
        c.wait_send()
    for c in feat_copies[1]:
        c.start()
    lax.fori_loop(4, K, build, 0)

    in_copies[4].wait()
    rows_to_lanes(raw.at[1], cot)

    theirs = pl.ds(pl.multiple_of(128 * (1 - core), 128), 128)
    mine = pl.ds(pl.multiple_of(128 * core, 128), 128)

    def core_copy(h):
        cols = slice(*COLUMNS[h])
        return remote(cs.at[:, cols], cr.at[:, cols], c_ss.at[h], c_rs.at[h], sibling)

    def basis(h):
        hc = half_rows[h]
        for k in range(K):
            acc = dot(feat[hc, :], bmat[k, 1]) + dot(fx[0, hc, :], bmat[k, 0])
            acc += dot(fx[1, hc, :], bmat[k, 2]) + dot(e_rows[hc, :], bhal[k])
            rows = pl.ds(hc.start * K + k, hc.stop - hc.start, stride=K)
            big[0, rows, :] = acc[:, :LANES]
            big[1, rows, :] = acc[:, LANES:]
        for a in range(*COLUMNS[h], 256):
            rows = slice(a, a + 256)
            bo[rows, :LANES] = big[0, rows, :].astype(BF)
            bo[rows, LANES:] = big[1, rows, :].astype(BF)
            cs[:, rows] = dot(cot[theirs, :], bo[rows, :], NT).astype(BF)
        core_copy(h).start()

    def weight_rows(h):
        for a in range(*COLUMNS[h], 256):
            own[:, a : a + 256] = dot(cot[mine, :], bo[a : a + 256, :], NT)

    def xy_copy(h, i):
        src, dst = xs.at[xy_index(i), PIECE[h]], xr.at[i, PIECE[h]]
        return remote(src, dst, x_ss.at[h, i], x_rs.at[h, i], xy_peer(i))

    def z_copy(h, i, n):
        ref = zr.at[n, PIECE[h]]
        return remote(ref, ref, z_ss.at[h, i], z_rs.at[h, i], z_peer(i))

    def gx_copy(h, i, n):
        ref = ga.at[core, n, PIECE[h]]
        return remote(ref, ref, gx_ss.at[h, i], gx_rs.at[h, i], xy_peer(i))

    def gc_copy(h, i, c):
        ref = ga.at[c, from_index(i), PIECE[h]]
        return remote(ref, ref, gc_ss.at[h, i], gc_rs.at[h, i], sibling)

    def sent(copy, order, *args):
        for i in order:
            copy(0, i, *args).wait_send()

    def core_sum(h):
        core_copy(h).wait()
        cols = slice(*COLUMNS[h])
        v = own[:, cols] + cr[:, cols].astype(F32)
        tiles = [v[:, a : a + LANES].reshape(16, 8, LANES) for a in range(0, v.shape[1], LANES)]
        for m in range(0, len(tiles), 2):
            rows = slice(PIECE[h].start + 8 * m, PIECE[h].start + 8 * m + 16)
            xs[:, rows, :] = jnp.concatenate(tiles[m : m + 2], axis=1).astype(BF)
        for i in reversed(NEAR_FIRST):
            xy_copy(h, i).start()

    def sum_xy(h):
        total = xs[me_n, PIECE[h], :].astype(F32)
        for i in NEAR_FIRST:
            xy_copy(h, i).wait_recv()
            total += xr[i, PIECE[h], :].astype(F32)
        zr[z, PIECE[h], :] = total.astype(BF)
        if h == 1:
            sent(z_copy, Z_FAR_FIRST, z)
        for i in Z_FAR_FIRST:
            z_copy(h, i, z).start()

    def sum_z(h):
        for i in range(1, NZ):
            z_copy(h, i, (z + 8 - i) % 8).wait_recv()
        total = zr[0, PIECE[h], :].astype(F32)
        for i in range(1, NZ):
            total += zr[i, PIECE[h], :].astype(F32)
        total *= F32(1.0 / math.sqrt(N_ROWS * N_LON * LANES))
        ga[core, me_n, PIECE[h], :] = total.astype(BF)
        gc_copy(h, 0, core).start()
        if h == 1:
            sent(gx_copy, NEAR_FIRST, me_n)
        for i in reversed(NEAR_FIRST):
            gx_copy(h, i, me_n).start()
        widen(h, core, me_n)

    def widen(h, c, n):
        v = ga[c, n, PIECE[h], :].astype(F32)
        rows = pl.ds(pl.multiple_of(128 * c + 8 * n, 8), 8)
        for m in range(v.shape[0] // 8):
            a = COLUMNS[h][0] + m * LANES
            wg[rows, a : a + LANES] = v[8 * m : 8 * m + 8]

    def gather_xy(h):
        for i in NEAR_FIRST:
            n = from_index(i)
            gx_copy(h, i, n).wait_recv()
            gc_copy(h, i, core).start()
        for i in NEAR_FIRST:
            widen(h, core, from_index(i))

    def gather_core(h):
        for i in [0] + NEAR_FIRST:
            gc_copy(h, i, 1 - core).wait_recv()
            widen(h, 1 - core, from_index(i))

    for c in feat_copies[0]:
        c.wait_recv()
    for c in edge_copies:
        c.wait()
    e_rows[...] = jnp.transpose(e_recv[...].reshape(96, C).astype(F32)).astype(BF)
    basis(0)
    weight_rows(0)
    core_sum(0)
    for c in feat_copies[1]:
        c.wait()
    basis(1)
    weight_rows(1)
    core_sum(1)

    in_copies[5].wait()

    def basis_grad(m, _):
        cols = pl.ds(pl.multiple_of(m * 256, 256), 256)
        g = dot(w[:, cols], cot[...], TN)
        big[0, cols, :] = g[:, :LANES]
        big[1, cols, :] = g[:, LANES:]
        return 0

    lax.fori_loop(0, K, basis_grad, 0)
    for k in range(K):
        for t in range(2):
            bgk[k, :, t * LANES : (t + 1) * LANES] = big[t, pl.ds(k, C, stride=K), :].astype(BF)

    def input_grad(dl):
        acc = dot(bgk[0], bmat[0, dl], NT)
        for k in range(1, K):
            acc += dot(bgk[k], bmat[k, dl], NT)
        return acc

    igp[0] = input_grad(0).astype(BF)
    sum_xy(0)
    igp[1] = input_grad(2).astype(BF)
    acc = dot(bhal[0], bgk[0], NT)
    for k in range(1, K):
        acc += dot(bhal[k], bgk[k], NT)
    for s in range(6):
        egs[s] = acc[s * 16 : s * 16 + 16].astype(BF)
    grad_copies = [
        remote(igp.at[0], gr.at[1], g_ss.at[0], g_rs.at[1], lat_peer(-1)),
        remote(igp.at[1], gr.at[0], g_ss.at[1], g_rs.at[0], lat_peer(1)),
    ] + [remote(egs.at[s], egr.at[s], h_ss.at[s], h_rs.at[s], edge_peer(s)) for s in range(6)]
    for c in grad_copies:
        c.start()
    igo[...] = input_grad(1)
    sum_xy(1)

    acc = dot(w[:, :256], bo[:256, :])
    for m in range(1, K):
        acc += dot(w[:, m * 256 : m * 256 + 256], bo[m * 256 : m * 256 + 256, :])
    out[...] = lanes_to_rows(acc)
    sum_z(0)
    sum_z(1)
    gather_xy(0)

    for c in grad_copies:
        c.wait()
    edges = egr[0].astype(F32)
    for s in range(1, 6):
        edges += egr[s].astype(F32)
    acc = igo[...] + gr[0].astype(F32) + gr[1].astype(F32)
    edge_hi = edges.astype(BF)
    edge_lo = (edges - edge_hi.astype(F32)).astype(BF)
    acc += dot(edge_hi, sel, TN) + dot(edge_lo, sel, TN)
    ig[...] = lanes_to_rows(acc)

    gather_core(0)
    gather_xy(1)
    gather_core(1)
    for i in NEAR_FIRST:
        xy_copy(0, i).wait_send()
        xy_copy(1, i).wait_send()
        gx_copy(1, i, me_n).wait_send()
    for i in Z_FAR_FIRST:
        z_copy(1, i, z).wait_send()
    for h in range(2):
        for i in [0] + NEAR_FIRST:
            gc_copy(h, i, core).wait_send()


def write_back(out_v, ig_v, wg_v, out, ig, wg, sem):
    copies = [
        pltpu.make_async_copy(wg_v.at[n : n + 64], wg.at[n : n + 64], sem.at[n // 64])
        for n in range(0, C, 64)
    ]
    copies.append(pltpu.make_async_copy(out_v, out, sem.at[4]))
    copies.append(pltpu.make_async_copy(ig_v, ig, sem.at[5]))
    for c in copies:
        c.start()
    for c in copies:
        c.wait()


def per_device(features, weight, filter_table, row_range, basis_id, cotangent):
    vmem = pl.BlockSpec(memory_space=pltpu.VMEM)
    hbm = pl.BlockSpec(memory_space=pltpu.HBM)
    dma = pltpu.SemaphoreType.DMA
    scratch = [
        pltpu.VMEM((2, C, 2, LANES), BF),
        pltpu.VMEM((C, 256), BF),
        pltpu.VMEM((C, 256), BF),
        pltpu.SMEM((K, 5, 16), F32),
        pltpu.SMEM((2, N_ROWS), jnp.int32),
        pltpu.SMEM((5, N_ROWS), jnp.int32),
        pltpu.VMEM((C, C * K), BF),
        pltpu.VMEM((2, C, 256), BF),
        pltpu.VMEM((16, C), BF),
        pltpu.VMEM((6, 16, C), BF),
        pltpu.VMEM((C, 96), BF),
        pltpu.VMEM((K, 3, 256, 256), BF),
        pltpu.VMEM((K, 96, 256), BF),
        pltpu.VMEM((2, C * K, LANES), F32),
        pltpu.VMEM((C * K, 256), BF),
        pltpu.VMEM((K, C, 256), BF),
        pltpu.VMEM((2, C, 256), BF),
        pltpu.VMEM((2, C, 256), BF),
        pltpu.VMEM((6, 16, C), BF),
        pltpu.VMEM((6, 16, C), BF),
        pltpu.VMEM((128, C * K), BF),
        pltpu.VMEM((128, C * K), BF),
        pltpu.VMEM((128, C * K), F32),
        pltpu.VMEM((16, 144, LANES), BF),
        pltpu.VMEM((16, 144, LANES), BF),
        pltpu.VMEM((NZ, 144, LANES), BF),
        pltpu.VMEM((2, 16, 144, LANES), BF),
        pltpu.VMEM((C, 256), F32),
        dma((6,)),
        dma((2, 2)), dma((2, 2)), dma((6,)), dma((6,)), dma((2,)), dma((2,)), dma((6,)), dma((6,)),
        dma((2,)), dma((2,)),
        dma((2, 16)), dma((2, 16)), dma((2, NZ)), dma((2, NZ)),
        dma((2, 16)), dma((2, 16)), dma((2, 16)), dma((2, 16)),
    ]
    out, ig, wg = pl.pallas_call(
        kernel,
        out_shape=(
            pltpu.VMEM((C, 2, LANES), BF),
            pltpu.VMEM((C, 2, LANES), BF),
            pltpu.VMEM((C, C * K), F32),
        ),
        in_specs=[hbm] * 6,
        out_specs=(vmem, vmem, vmem),
        scratch_shapes=scratch,
        compiler_params=pltpu.CompilerParams(
            collective_id=0, has_side_effects=True, vmem_limit_bytes=56 * 1024 * 1024
        ),
    )(
        features,
        cotangent,
        weight,
        filter_table.transpose(1, 2, 0),
        row_range.T,
        basis_id.T,
    )
    return pl.pallas_call(
        write_back,
        out_shape=(
            jax.ShapeDtypeStruct((C, 2, LANES), BF),
            jax.ShapeDtypeStruct((C, 2, LANES), BF),
            jax.ShapeDtypeStruct((C, C * K), F32),
        ),
        in_specs=[vmem] * 3,
        out_specs=(hbm, hbm, hbm),
        scratch_shapes=[dma((6,))],
    )(*[pltpu.with_memory_space_constraint(v, pltpu.VMEM) for v in (out, ig, wg)])


def solution(mesh):
    in_specs = (P(None, "lat", "lon"), P(), P(), P(), P(), P(None, "lat", "lon"))
    out_specs = (P(None, "lat", "lon"), P(None, "lat", "lon"), P())
    return jax.shard_map(
        per_device, mesh=mesh, in_specs=in_specs, out_specs=out_specs, check_vma=False
    )
```

```python
import functools
import math

import jax
import jax.numpy as jnp
from jax import lax
from jax.experimental import pallas as pl
from jax.experimental.pallas import tpu as pltpu
from jax.sharding import PartitionSpec as P

BF = jnp.bfloat16
F32 = jnp.float32
MESH = pl.DeviceIdType.MESH
C = 256
K = 9
LANES = 128
NZ = 8
N_LAT, N_LON = 64, 4
N_ROWS = 128
CHANNELS = [(0, 144), (144, 256)]
COLUMNS = [(0, 1280), (1280, 2304)]
PIECE = [slice(0, 80), slice(80, 144)]
NEAR_FIRST = [1, 3, 4, 12, 5, 7, 13, 15, 2, 8, 6, 14, 9, 11, 10]
Z_FAR_FIRST = [4, 3, 5, 2, 6, 1, 7]
NT = (((1,), (1,)), ((), ()))
TN = (((0,), (0,)), ((), ()))
NN = (((1,), (0,)), ((), ()))


def dot(a, b, dims=NN):
    return lax.dot_general(a, b, dims, preferred_element_type=F32)


def kernel(
    feat_hbm, cot_hbm, w_hbm, table_hbm, rng_hbm, ids_hbm,
    out, ig, wg,
    raw, feat, cot, table, rng, ids, w, fx, e_send, e_recv, e_rows, bmat, bhal, big, bo, bgk, igp, gr, egs, egr,
    cs, cr, own, xs, xr, zr, ga, igo,
    in_sem, f_ss, f_rs, e_ss, e_rs, g_ss, g_rs, h_ss, h_rs, c_ss, c_rs,
    x_ss, x_rs, z_ss, z_rs, gx_ss, gx_rs, gc_ss, gc_rs,
):
    la, lo = lax.axis_index("lat"), lax.axis_index("lon")
    y, z, xh = la // 16, (la // 2) % 8, la % 2
    xl, core = lo // 2, lo % 2
    x = xh * 2 + xl
    sibling = (la, lo + 1 - 2 * core)
    me_n = y * 4 + x

    def lat_peer(dl):
        return (lax.rem(la + dl + N_LAT, N_LAT), lo)

    def edge_peer(s):
        dl, dc = s // 2 - 1, 2 * (s % 2) - 1
        return (lax.rem(la + dl + N_LAT, N_LAT), lax.rem(lo + dc + N_LON, N_LON))

    def plane(i, sign=1):
        return (y + 4 + sign * (i // 4)) % 4, (x + 4 + sign * (i % 4)) % 4

    def xy_peer(i):
        py, px = plane(i)
        return ((py * 8 + z) * 2 + px // 2, (px % 2) * 2 + core)

    def xy_index(i):
        py, px = plane(i)
        return py * 4 + px

    def from_index(i):
        py, px = plane(i, -1)
        return py * 4 + px

    def z_peer(i):
        return ((y * 8 + (z + i) % 8) * 2 + xh, lo)

    in_copies = [
        pltpu.make_async_copy(src, dst, in_sem.at[i])
        for i, (src, dst) in enumerate(
            [
                (feat_hbm, raw.at[0]),
                (table_hbm, table),
                (rng_hbm, rng),
                (ids_hbm, ids),
                (cot_hbm, raw.at[1]),
                (w_hbm, w),
            ]
        )
    ]
    for c in in_copies:
        c.start()

    barrier = pltpu.get_barrier_semaphore()
    peers = [lat_peer(-1), lat_peer(1)] + [edge_peer(s) for s in range(6)]
    peers += [xy_peer(i) for i in NEAR_FIRST if i != 2]
    peers += [z_peer(i) for i in range(1, NZ)]
    for peer in peers:
        pl.semaphore_signal(barrier, inc=1, device_id=peer, device_id_type=MESH)

    def rows_to_lanes(ref, dst):
        v = ref[...].astype(F32)
        dst[:, :LANES] = v[:, 0, :].astype(BF)
        dst[:, LANES:] = v[:, 1, :].astype(BF)

    def lanes_to_rows(v):
        return jnp.stack([v[:, :LANES], v[:, LANES:]], axis=1).astype(BF)

    in_copies[0].wait()
    rows_to_lanes(raw.at[0], feat)

    rho = lax.broadcasted_iota(jnp.int32, (16, 2 * LANES), 0)
    col = lax.broadcasted_iota(jnp.int32, (16, 2 * LANES), 1)
    edge_i = rho % 4
    edge_col = jnp.where(edge_i < 2, edge_i, edge_i + LANES - 4)
    sel = ((rho < 8) & (col == (rho // 4) * LANES + edge_col)).astype(F32).astype(BF)
    e_send[...] = dot(sel, feat[...], NT).astype(BF)

    pl.semaphore_wait(barrier, len(peers))

    def remote(src, dst, ss, rs, peer):
        return pltpu.make_async_remote_copy(
            src_ref=src, dst_ref=dst, send_sem=ss, recv_sem=rs, device_id=peer, device_id_type=MESH
        )

    half_rows = [slice(*c) for c in CHANNELS]
    feat_copies = [
        [
            remote(
                feat.at[half_rows[h]], fx.at[1, half_rows[h]], f_ss.at[h, 0], f_rs.at[h, 1], lat_peer(-1)
            ),
            remote(
                feat.at[half_rows[h]], fx.at[0, half_rows[h]], f_ss.at[h, 1], f_rs.at[h, 0], lat_peer(1)
            ),
        ]
        for h in range(2)
    ]
    edge_copies = [
        remote(e_send, e_recv.at[5 - s], e_ss.at[s], e_rs.at[5 - s], edge_peer(s)) for s in range(6)
    ]
    for c in feat_copies[0] + edge_copies:
        c.start()

    for c in in_copies[1:4]:
        c.wait()
    diag = lax.broadcasted_iota(jnp.int32, (LANES, LANES), 0) - lax.broadcasted_iota(
        jnp.int32, (LANES, LANES), 1
    ) + 2
    hr = lax.broadcasted_iota(jnp.int32, (16, LANES), 0)
    hp = lax.broadcasted_iota(jnp.int32, (16, LANES), 1)
    row_ids, row_act = [], []
    for t in range(2):
        g = la * 2 + t
        r0, r1_ = rng[0, g], rng[1, g]
        row_ids.append([ids[j, g] for j in range(5)])
        row_act.append(
            [
                (j >= r0) & (j < r1_) & (g + j - 2 >= 0) & (g + j - 2 < N_ROWS)
                for j in range(5)
            ]
        )
    zero_block = jnp.zeros((LANES, LANES), BF)

    def build(k, _):
        coef = [
            [
                [jnp.where(row_act[t][j], table[k, l, row_ids[t][j]], 0.0) for l in range(5)]
                for j in range(5)
            ]
            for t in range(2)
        ]
        for t in range(2):
            lanes = slice(t * LANES, (t + 1) * LANES)
            for e in range(6):
                j = e - t
                rows = slice((e % 2) * LANES, (e % 2 + 1) * LANES)
                if j < 0 or j > 4:
                    bmat[k, e // 2, rows, lanes] = zero_block
                    continue
                v = jnp.zeros((LANES, LANES), F32)
                for l in range(5):
                    v = jnp.where(diag == l, coef[t][j][l], v)
                bmat[k, e // 2, rows, lanes] = v.astype(BF)
            for s in range(6):
                v = jnp.zeros((16, LANES), F32)
                for r in range(2):
                    j = (s // 2) * 2 + r - t
                    if j < 0 or j > 4:
                        continue
                    if s % 2 == 0:
                        outer = (hr == r * 4 + 2) & (hp == 0) | (hr == r * 4 + 3) & (hp == 1)
                        inner = (hr == r * 4 + 3) & (hp == 0)
                        v = jnp.where(outer, coef[t][j][0], jnp.where(inner, coef[t][j][1], v))
                    else:
                        outer = (hr == r * 4) & (hp == 126) | (hr == r * 4 + 1) & (hp == 127)
                        inner = (hr == r * 4) & (hp == 127)
                        v = jnp.where(outer, coef[t][j][4], jnp.where(inner, coef[t][j][3], v))
                bhal[k, s * 16 : s * 16 + 16, lanes] = v.astype(BF)
        return 0

    lax.fori_loop(0, 4, build, 0)
    for c in feat_copies[0]:
        c.wait_send()
    for c in feat_copies[1]:
        c.start()
    lax.fori_loop(4, K, build, 0)

    in_copies[4].wait()
    rows_to_lanes(raw.at[1], cot)

    theirs = pl.ds(pl.multiple_of(128 * (1 - core), 128), 128)
    mine = pl.ds(pl.multiple_of(128 * core, 128), 128)

    def core_copy(h):
        cols = slice(*COLUMNS[h])
        return remote(cs.at[:, cols], cr.at[:, cols], c_ss.at[h], c_rs.at[h], sibling)

    def basis(h):
        hc = half_rows[h]
        for k in range(K):
            acc = dot(feat[hc, :], bmat[k, 1]) + dot(fx[0, hc, :], bmat[k, 0])
            acc += dot(fx[1, hc, :], bmat[k, 2]) + dot(e_rows[hc, :], bhal[k])
            rows = pl.ds(hc.start * K + k, hc.stop - hc.start, stride=K)
            big[0, rows, :] = acc[:, :LANES]
            big[1, rows, :] = acc[:, LANES:]
        for a in range(*COLUMNS[h], 256):
            rows = slice(a, a + 256)
            bo[rows, :LANES] = big[0, rows, :].astype(BF)
            bo[rows, LANES:] = big[1, rows, :].astype(BF)
            cs[:, rows] = dot(cot[theirs, :], bo[rows, :], NT).astype(BF)
        core_copy(h).start()

    def weight_rows(h):
        for a in range(*COLUMNS[h], 256):
            own[:, a : a + 256] = dot(cot[mine, :], bo[a : a + 256, :], NT)

    def xy_copy(h, i):
        src, dst = xs.at[xy_index(i), PIECE[h]], xr.at[i, PIECE[h]]
        return remote(src, dst, x_ss.at[h, i], x_rs.at[h, i], xy_peer(i))

    def z_copy(h, i, n):
        ref = zr.at[n, PIECE[h]]
        return remote(ref, ref, z_ss.at[h, i], z_rs.at[h, i], z_peer(i))

    def gx_copy(h, i, n):
        ref = ga.at[core, n, PIECE[h]]
        return remote(ref, ref, gx_ss.at[h, i], gx_rs.at[h, i], xy_peer(i))

    def gc_copy(h, i, c):
        ref = ga.at[c, from_index(i), PIECE[h]]
        return remote(ref, ref, gc_ss.at[h, i], gc_rs.at[h, i], sibling)

    def sent(copy, order, *args):
        for i in order:
            copy(0, i, *args).wait_send()

    def core_sum(h):
        core_copy(h).wait()
        cols = slice(*COLUMNS[h])
        v = own[:, cols] + cr[:, cols].astype(F32)
        tiles = [v[:, a : a + LANES].reshape(16, 8, LANES) for a in range(0, v.shape[1], LANES)]
        for m in range(0, len(tiles), 2):
            rows = slice(PIECE[h].start + 8 * m, PIECE[h].start + 8 * m + 16)
            xs[:, rows, :] = jnp.concatenate(tiles[m : m + 2], axis=1).astype(BF)
        for i in reversed(NEAR_FIRST):
            xy_copy(h, i).start()

    def sum_xy(h):
        total = xs[me_n, PIECE[h], :].astype(F32)
        for i in NEAR_FIRST:
            xy_copy(h, i).wait_recv()
            total += xr[i, PIECE[h], :].astype(F32)
        zr[z, PIECE[h], :] = total.astype(BF)
        if h == 1:
            sent(z_copy, Z_FAR_FIRST, z)
        for i in Z_FAR_FIRST:
            z_copy(h, i, z).start()

    def sum_z(h):
        for i in range(1, NZ):
            z_copy(h, i, (z + 8 - i) % 8).wait_recv()
        total = zr[0, PIECE[h], :].astype(F32)
        for i in range(1, NZ):
            total += zr[i, PIECE[h], :].astype(F32)
        total *= F32(1.0 / math.sqrt(N_ROWS * N_LON * LANES))
        ga[core, me_n, PIECE[h], :] = total.astype(BF)
        gc_copy(h, 0, core).start()
        if h == 1:
            sent(gx_copy, NEAR_FIRST, me_n)
        for i in reversed(NEAR_FIRST):
            gx_copy(h, i, me_n).start()
        widen(h, core, me_n)

    def widen(h, c, n):
        v = ga[c, n, PIECE[h], :].astype(F32)
        rows = pl.ds(pl.multiple_of(128 * c + 8 * n, 8), 8)
        for m in range(v.shape[0] // 8):
            a = COLUMNS[h][0] + m * LANES
            wg[rows, a : a + LANES] = v[8 * m : 8 * m + 8]

    def gather_xy(h):
        for i in NEAR_FIRST:
            n = from_index(i)
            gx_copy(h, i, n).wait_recv()
            gc_copy(h, i, core).start()
        for i in NEAR_FIRST:
            widen(h, core, from_index(i))

    def gather_core(h):
        for i in [0] + NEAR_FIRST:
            gc_copy(h, i, 1 - core).wait_recv()
            widen(h, 1 - core, from_index(i))

    for c in feat_copies[0]:
        c.wait_recv()
    for c in edge_copies:
        c.wait()
    e_rows[...] = jnp.transpose(e_recv[...].reshape(96, C).astype(F32)).astype(BF)
    basis(0)
    weight_rows(0)
    core_sum(0)
    for c in feat_copies[1]:
        c.wait()
    basis(1)
    weight_rows(1)
    core_sum(1)

    in_copies[5].wait()

    def basis_grad(m, _):
        cols = pl.ds(pl.multiple_of(m * 256, 256), 256)
        g = dot(w[:, cols], cot[...], TN)
        big[0, cols, :] = g[:, :LANES]
        big[1, cols, :] = g[:, LANES:]
        return 0

    lax.fori_loop(0, K, basis_grad, 0)
    for k in range(K):
        for t in range(2):
            bgk[k, :, t * LANES : (t + 1) * LANES] = big[t, pl.ds(k, C, stride=K), :].astype(BF)

    def input_grad(dl):
        acc = dot(bgk[0], bmat[0, dl], NT)
        for k in range(1, K):
            acc += dot(bgk[k], bmat[k, dl], NT)
        return acc

    igp[0] = input_grad(0).astype(BF)
    sum_xy(0)
    igp[1] = input_grad(2).astype(BF)
    acc = dot(bhal[0], bgk[0], NT)
    for k in range(1, K):
        acc += dot(bhal[k], bgk[k], NT)
    for s in range(6):
        egs[s] = acc[s * 16 : s * 16 + 16].astype(BF)
    grad_copies = [
        remote(igp.at[0], gr.at[1], g_ss.at[0], g_rs.at[1], lat_peer(-1)),
        remote(igp.at[1], gr.at[0], g_ss.at[1], g_rs.at[0], lat_peer(1)),
    ] + [remote(egs.at[s], egr.at[s], h_ss.at[s], h_rs.at[s], edge_peer(s)) for s in range(6)]
    for c in grad_copies:
        c.start()
    igo[...] = input_grad(1)
    sum_xy(1)

    acc = dot(w[:, :256], bo[:256, :])
    for m in range(1, K):
        acc += dot(w[:, m * 256 : m * 256 + 256], bo[m * 256 : m * 256 + 256, :])
    out[...] = lanes_to_rows(acc)
    sum_z(0)
    sum_z(1)
    gather_xy(0)

    for c in grad_copies:
        c.wait()
    edges = egr[0].astype(F32)
    for s in range(1, 6):
        edges += egr[s].astype(F32)
    acc = igo[...] + gr[0].astype(F32) + gr[1].astype(F32)
    edge_hi = edges.astype(BF)
    edge_lo = (edges - edge_hi.astype(F32)).astype(BF)
    acc += dot(edge_hi, sel, TN) + dot(edge_lo, sel, TN)
    ig[...] = lanes_to_rows(acc)

    gather_xy(1)
    gather_core(0)
    gather_core(1)
    for i in NEAR_FIRST:
        xy_copy(0, i).wait_send()
        xy_copy(1, i).wait_send()
        gx_copy(1, i, me_n).wait_send()
    for i in Z_FAR_FIRST:
        z_copy(1, i, z).wait_send()
    for h in range(2):
        for i in [0] + NEAR_FIRST:
            gc_copy(h, i, core).wait_send()


def write_back(out_v, ig_v, wg_v, out, ig, wg, sem):
    copies = [
        pltpu.make_async_copy(wg_v.at[n : n + 64], wg.at[n : n + 64], sem.at[n // 64])
        for n in range(0, C, 64)
    ]
    copies.append(pltpu.make_async_copy(out_v, out, sem.at[4]))
    copies.append(pltpu.make_async_copy(ig_v, ig, sem.at[5]))
    for c in copies:
        c.start()
    for c in copies:
        c.wait()


def per_device(features, weight, filter_table, row_range, basis_id, cotangent):
    vmem = pl.BlockSpec(memory_space=pltpu.VMEM)
    hbm = pl.BlockSpec(memory_space=pltpu.HBM)
    dma = pltpu.SemaphoreType.DMA
    scratch = [
        pltpu.VMEM((2, C, 2, LANES), BF),
        pltpu.VMEM((C, 256), BF),
        pltpu.VMEM((C, 256), BF),
        pltpu.SMEM((K, 5, 16), F32),
        pltpu.SMEM((2, N_ROWS), jnp.int32),
        pltpu.SMEM((5, N_ROWS), jnp.int32),
        pltpu.VMEM((C, C * K), BF),
        pltpu.VMEM((2, C, 256), BF),
        pltpu.VMEM((16, C), BF),
        pltpu.VMEM((6, 16, C), BF),
        pltpu.VMEM((C, 96), BF),
        pltpu.VMEM((K, 3, 256, 256), BF),
        pltpu.VMEM((K, 96, 256), BF),
        pltpu.VMEM((2, C * K, LANES), F32),
        pltpu.VMEM((C * K, 256), BF),
        pltpu.VMEM((K, C, 256), BF),
        pltpu.VMEM((2, C, 256), BF),
        pltpu.VMEM((2, C, 256), BF),
        pltpu.VMEM((6, 16, C), BF),
        pltpu.VMEM((6, 16, C), BF),
        pltpu.VMEM((128, C * K), BF),
        pltpu.VMEM((128, C * K), BF),
        pltpu.VMEM((128, C * K), F32),
        pltpu.VMEM((16, 144, LANES), BF),
        pltpu.VMEM((16, 144, LANES), BF),
        pltpu.VMEM((NZ, 144, LANES), BF),
        pltpu.VMEM((2, 16, 144, LANES), BF),
        pltpu.VMEM((C, 256), F32),
        dma((6,)),
        dma((2, 2)), dma((2, 2)), dma((6,)), dma((6,)), dma((2,)), dma((2,)), dma((6,)), dma((6,)),
        dma((2,)), dma((2,)),
        dma((2, 16)), dma((2, 16)), dma((2, NZ)), dma((2, NZ)),
        dma((2, 16)), dma((2, 16)), dma((2, 16)), dma((2, 16)),
    ]
    out, ig, wg = pl.pallas_call(
        kernel,
        out_shape=(
            pltpu.VMEM((C, 2, LANES), BF),
            pltpu.VMEM((C, 2, LANES), BF),
            pltpu.VMEM((C, C * K), F32),
        ),
        in_specs=[hbm] * 6,
        out_specs=(vmem, vmem, vmem),
        scratch_shapes=scratch,
        compiler_params=pltpu.CompilerParams(
            collective_id=0, has_side_effects=True, vmem_limit_bytes=56 * 1024 * 1024
        ),
    )(
        features,
        cotangent,
        weight,
        filter_table.transpose(1, 2, 0),
        row_range.T,
        basis_id.T,
    )
    return pl.pallas_call(
        write_back,
        out_shape=(
            jax.ShapeDtypeStruct((C, 2, LANES), BF),
            jax.ShapeDtypeStruct((C, 2, LANES), BF),
            jax.ShapeDtypeStruct((C, C * K), F32),
        ),
        in_specs=[vmem] * 3,
        out_specs=(hbm, hbm, hbm),
        scratch_shapes=[dma((6,))],
    )(*[pltpu.with_memory_space_constraint(v, pltpu.VMEM) for v in (out, ig, wg)])


def solution(mesh):
    in_specs = (P(None, "lat", "lon"), P(), P(), P(), P(), P(None, "lat", "lon"))
    out_specs = (P(None, "lat", "lon"), P(None, "lat", "lon"), P())
    return jax.shard_map(
        per_device, mesh=mesh, in_specs=in_specs, out_specs=out_specs, check_vma=False
    )
```
